32 devices in a mesh: segment: 2 (over y), win: 4 (over z), seq: 4 (over x, core).
Axes of the slice: x: 2, y: 2, z: 4, core: 2. Of those that a mesh axis runs over, the one named last changes fastest.
Arguments:
- latents: bfloat16 [2, 32, 128, 1536], P('segment', 'seq', 'win'), may hold values from -6 to 6
- timesteps: int32 [2], P('segment'), may hold values from 0 to 31, as said below
- offsets: int32 [2, 2], P('segment'), may hold values from 1 to 31
- qkv_weight: bfloat16 [2, 1536, 16, 288], P('segment', None, 'seq'), may hold values from -0.15309311 to 0.15309311
- logit_scale: float32 [2, 16], P('segment', 'seq'), may hold values from 4 to 256
- out_weight: bfloat16 [2, 1536, 1536], P('segment'), may hold values from -0.15625 to 0.15625
- mod_shift: float32 [2, 32, 1536], P('segment'), may hold values from -3 to 3
- mod_scale: float32 [2, 32, 1536], P('segment'), may hold values from 0.5 to 1.5
- mod_gate: float32 [2, 32, 1536], P('segment'), may hold values from 1 to 3
Outputs:
- handed: bfloat16 [2, 32, 128, 1536], P('segment', 'seq', 'win')
The draws below stay inside these ranges and needn't reach their ends.
Inputs may be any that keep to these rules, and one draw needn't show every extreme that they name: `timesteps`: the sections' noise levels differ from one another.
All inputs are finite; a program needn't handle non-finite values.
Results may differ from the reference program's by a relative error of at most 0.015.
Values may be sent and summed in bfloat16 or wider, within the bound.
No kernel may reach another device: no remote copies, remote signals or barrier semaphores. Data moves between devices by JAX's collectives and lax.ppermute only.
A program may use at most 64 MiB of HBM per device.

```python
import jax
import jax.numpy as jnp
from jax import lax

D = 1536
HEADS = 16
HD = 96
WS = 32
STEPS = 32
SECTIONS = 2
HEAD_DEV = 4
LON = 128
N_SEQ = 4


def draw_timesteps(key, part):
    order = jax.random.permutation(jax.random.fold_in(key, 29), STEPS)
    return order[:SECTIONS].astype(jnp.int32)


def draw_logit_scale(key, part):
    lows = jnp.exp(jax.random.uniform(jax.random.fold_in(key, 11), (SECTIONS, HEADS), jnp.float32, jnp.log(4.0), jnp.log(24.0)))
    return lows


def draw_qkv_weight(key, part):
    shape = (SECTIONS, D, HEADS, 3 * HD)
    spread = D ** (-0.5)
    normal = jax.random.normal(jax.random.fold_in(key, 17), shape, jnp.float32) * spread
    return jnp.clip(normal, -6.0 * spread, 6.0 * spread).astype(jnp.bfloat16)


def draw_latents(key, part):
    shape = (SECTIONS, WS, LON, D)
    return jnp.clip(jax.random.normal(jax.random.fold_in(key, 19), shape, jnp.float32), -6.0, 6.0).astype(jnp.bfloat16)


def place_ends(entries, rng, smallest, high):
    dims = entries.shape
    spot = [jax.random.randint(jax.random.fold_in(rng, axis), (), 0, dims[axis]) for axis in range(len(dims))]
    entries = entries.at[tuple(spot)].set(smallest)
    longest = dims.index(max(dims))
    spot[longest] = (spot[longest] + 1) % dims[longest]
    return entries.at[tuple(spot)].set(high)


def block_scale(own_key, dims, cuts, low, top_value):
    def one(axis_at, blocks):
        heights = jax.random.uniform(jax.random.fold_in(jax.random.fold_in(own_key, 6), axis_at), (blocks,), jnp.float32, low / len(cuts), top_value / len(cuts))
        return jnp.repeat(jnp.exp(heights), dims[axis_at] // blocks).reshape((-1,) + (1,) * (len(dims) - axis_at - 1))

    level = one(*cuts[0])
    for cut in cuts[1:]:
        level = level * one(*cut)
    return level


def bell_draw(key, extent, scale, bound, shards=(), kind=jnp.bfloat16):
    gain = block_scale(key, extent, shards, -0.22, 0.18) if shards else 1.0
    drawn = jax.random.normal(key, extent, jnp.float32) * scale * gain
    return jnp.minimum(jnp.maximum(drawn, -bound), bound).astype(kind)


def setup_inputs(seed: int = 0) -> dict:
    arg_keys = jax.random.split(jax.random.key(seed), 10)
    latents = draw_latents(jax.random.fold_in(arg_keys[9], 71), 0)
    timesteps = draw_timesteps(jax.random.fold_in(arg_keys[9], 71), 0)
    offsets = place_ends(jax.random.randint(arg_keys[2], (SECTIONS, 2), 1, WS), jax.random.fold_in(arg_keys[2], 1), 1, WS - 1).astype(jnp.int32)
    qkv_weight = draw_qkv_weight(jax.random.fold_in(arg_keys[9], 71), 0)
    logit_scale = draw_logit_scale(jax.random.fold_in(arg_keys[9], 71), 0)
    out_weight = bell_draw(arg_keys[5], (SECTIONS, HEADS * HD, D), (HEADS * HD) ** -0.5, 0.15625, ((0, 2),))
    mod_shift = bell_draw(arg_keys[6], (SECTIONS, STEPS, D), 0.5, 3.0, ((0, 2),), jnp.float32)
    mod_scale = jnp.clip(1.0 + 0.1 * jax.random.normal(arg_keys[7], (SECTIONS, STEPS, D), jnp.float32), 0.5, 1.5)
    mod_gate = jnp.clip(1.0 + 2.0 * jax.random.uniform(arg_keys[8], (SECTIONS, STEPS, D), jnp.float32) ** block_scale(arg_keys[8], (SECTIONS, STEPS, D), ((0, 2),), -0.2, 0.2), 1.0, 3.0)
    return dict(latents=latents, timesteps=timesteps, offsets=offsets, qkv_weight=qkv_weight, logit_scale=logit_scale, out_weight=out_weight, mod_shift=mod_shift, mod_scale=mod_scale, mod_gate=mod_gate)


eps_norm = 1e-06
masked = -1e+30

def unit_split(mixture, size):
    queries = mixture[..., :size]
    key_part = mixture[..., size:2 * size]
    values = mixture[..., 2 * size:]
    queries = queries * lax.rsqrt(lax.optimization_barrier(jnp.sum(queries * queries, -1, keepdims=True)) + eps_norm)
    key_part = key_part * lax.rsqrt(lax.optimization_barrier(jnp.sum(key_part * key_part, -1, keepdims=True)) + eps_norm)
    return jnp.concatenate([queries, key_part, values], -1).astype(jnp.bfloat16)

def table_row(table, noise_level):
    onehot = (jnp.arange(STEPS, dtype=jnp.int32) == noise_level).astype(jnp.float32)
    return jnp.dot(onehot, table, precision=lax.Precision.HIGHEST, preferred_element_type=jnp.float32)

def reference(latents, timesteps, offsets, qkv_weight, logit_scale, out_weight, mod_shift, mod_scale, mod_gate):
    results = []
    for section in range(SECTIONS):
        shift_row = table_row(mod_shift[section], timesteps[section])
        scale_row = table_row(mod_scale[section], timesteps[section])
        gate_row = table_row(mod_gate[section], timesteps[section])
        lat_offset = offsets[section, 0]
        lon_offset = offsets[section, 1]
        rolled = jnp.roll(latents[section], (-lat_offset, -lon_offset), axis=(0, 1))
        residual = rolled.astype(jnp.float32)
        average = lax.optimization_barrier(jnp.mean(residual, -1, keepdims=True))
        centred = residual - average
        variance = lax.optimization_barrier(jnp.mean(centred * centred, -1, keepdims=True))
        normed = (centred * lax.rsqrt(variance + eps_norm) * scale_row + shift_row).astype(jnp.bfloat16)
        windows = normed.reshape(WS, LON // WS, WS, D).transpose(1, 0, 2, 3)
        token_group = jnp.arange(WS * WS, dtype=jnp.int32) // WS >= WS - lat_offset
        allowed = token_group[:, None] == token_group[None, :]
        weights = qkv_weight[section].reshape(D, HEADS * 3 * HD)
        scales = logit_scale[section]
        grouped_out = out_weight[section].reshape(N_SEQ, HEAD_DEV * HD, D).astype(jnp.float32)

        def window_attend(window_tokens):
            flattened = window_tokens.reshape(WS * WS, D)
            mixture = jnp.dot(flattened, weights, preferred_element_type=jnp.float32).reshape(WS * WS, HEADS, 3 * HD)
            unit_heads = unit_split(mixture, HD).astype(jnp.float32)
            query_unit = unit_heads[..., :HD]
            key_unit = unit_heads[..., HD:2 * HD]
            value_rows = unit_heads[..., 2 * HD:]
            scores = jnp.einsum('qhd,khd->hqk', query_unit, key_unit, precision=lax.Precision.HIGHEST) * scales[:, None, None]
            scores = jnp.where(allowed[None], scores, masked)
            row_max = lax.optimization_barrier(jnp.max(scores, -1, keepdims=True))
            lifted = jnp.exp(scores - row_max)
            probabilities = (lifted / lax.optimization_barrier(jnp.sum(lifted, -1, keepdims=True))).astype(jnp.bfloat16)
            heads_out = jnp.einsum('hqk,khd->qhd', probabilities.astype(jnp.float32), value_rows, precision=lax.Precision.HIGHEST).astype(jnp.bfloat16)
            grouped = heads_out.reshape(WS * WS, N_SEQ, HEAD_DEV * HD).astype(jnp.float32)
            partial_value = jnp.einsum('tgk,gke->tge', grouped, grouped_out, precision=lax.Precision.HIGHEST).astype(jnp.bfloat16)
            return lax.optimization_barrier(jnp.sum(partial_value.astype(jnp.float32), 1)).astype(jnp.bfloat16).reshape(WS, WS, D)
        attention = lax.map(window_attend, windows)
        attention = attention.transpose(1, 0, 2, 3).reshape(WS, LON, D)
        updated = (residual + gate_row * attention.astype(jnp.float32)).astype(jnp.bfloat16)
        results.append(jnp.roll(updated, (lat_offset, lon_offset), axis=(0, 1)))
    stacked = jnp.stack(results)
    return jnp.roll(stacked, 1, axis=0)
```

```python
import functools
import math

import jax
import jax.numpy as jnp
from jax import lax
from jax.experimental import pallas as pl
from jax.experimental.pallas import tpu as pltpu
from jax.sharding import PartitionSpec as P

eps_norm = 1e-06
lane = 128
far = 1e30
constant_shift_scale = 32.0

SMEM = pl.BlockSpec(memory_space=pltpu.SMEM)
VMEM = pl.BlockSpec(memory_space=pltpu.VMEM)


small = pl.CostEstimate(flops=1, bytes_accessed=1, transcendentals=0)


def params(mib=40):
    return pltpu.CompilerParams(vmem_limit_bytes=mib << 20)


def passed_along(block, axis, distance):
    n = lax.axis_size(axis)
    return lax.ppermute(block, axis, [(i, (i + distance) % n) for i in range(n)])


def swapped(block, axis, mask):
    return lax.ppermute(block, axis, [(i, i ^ mask) for i in range(lax.axis_size(axis))])


def normalise(x, scale_row, shift_row):
    x = x - jnp.mean(x, -1, keepdims=True)
    variance = jnp.mean(x * x, -1, keepdims=True)
    return (x * lax.rsqrt(variance + eps_norm) * scale_row + shift_row).astype(jnp.bfloat16)


def local_half_kernel(ints, tile, shift, scale, out):
    rows, cols, _ = tile.shape
    half = cols // 2
    level, lon = ints[0], ints[2]
    first = pl.multiple_of(jnp.where(lon > half, 0, half), half)
    shift_row, scale_row = shift[pl.ds(level, 1), :], scale[pl.ds(level, 1), :]
    for r in range(rows):
        x = tile[r, pl.ds(first, half), :].astype(jnp.float32)
        out[r] = normalise(x, scale_row, shift_row)


def mixed_half(r, lon, tile, left, right):
    rows, cols, _ = tile.shape
    half = cols // 2
    big = lon > half
    first = pl.multiple_of(jnp.where(big, half, 0), half)
    column = lax.broadcasted_iota(jnp.int32, (half, 1), 0) + first
    far_side = jnp.where(big, (column >= lon).astype(jnp.int32), (column < lon).astype(jnp.int32)) == 1
    bigs = jnp.full((half, 1), lon, jnp.int32) > half
    own = tile[r, pl.ds(first, half), :].astype(jnp.float32)
    other = jnp.where(bigs, left[r].astype(jnp.float32), right[r].astype(jnp.float32))
    return jnp.where(far_side, other, own)


def mixed_half_kernel(ints, tile, left, right, shift, scale, out):
    rows = tile.shape[0]
    level, lon = ints[0], ints[2]
    shift_row, scale_row = shift[pl.ds(level, 1), :], scale[pl.ds(level, 1), :]
    for r in range(rows):
        x = mixed_half(r, lon, tile, left, right)
        out[r] = normalise(x, scale_row, shift_row)


def project_kernel(count, half, size, ints, places, fast, scales, *refs):
    pieces, weight, out = refs[:count], refs[count], refs[count + 1]
    tokens, padded, query_extra, key_extra = refs[count + 2 :]
    piece_rows = pieces[0].shape[0]
    group = weight.shape[0]
    total = tokens.shape[0]
    step = pl.program_id(0)

    @pl.when(step == 0)
    def _():
        padded[...] = jnp.zeros_like(padded)
        for j in range(count):
            tokens[pl.ds(pl.multiple_of(places[j] * piece_rows, piece_rows), piece_rows), :] = pieces[j][...]
        row = lax.broadcasted_iota(jnp.int32, (total, lane), 0) // half
        column = lax.broadcasted_iota(jnp.int32, (total, lane), 1)
        low = jnp.where(row < ints[1], 1.0, 0.0)
        query_extra[...] = jnp.where(
            column == size, low, jnp.where(column == size + 1, 1.0 - low, jnp.where(column == size + 2, 1.0, 0.0))
        )
        key_extra[...] = jnp.where(
            column == size,
            far * (low - 1.0),
            jnp.where(column == size + 1, -far * low, jnp.where(column == size + 2, -1.0, 0.0)),
        )

    for g in range(group):
        for i in range(3):
            begin = (3 * g + i) * lane
            padded[begin : begin + size, :] = weight[g, i * size : (i + 1) * size, :]
    mixture = lax.dot_general(
        tokens[...], padded[...], (((1,), (1,)), ((), ())), preferred_element_type=jnp.float32
    )
    ones = jnp.where(lax.broadcasted_iota(jnp.int32, (1, lane), 1) == size, 1.0, 0.0)
    for g in range(group):
        strength = jnp.where(fast[0] == 1, scales[step * group + g] * math.log2(math.e), 1.0)
        query, key, value = (mixture[:, (3 * g + i) * lane : (3 * g + i + 1) * lane] for i in range(3))
        query = query * (lax.rsqrt(jnp.sum(query * query, -1, keepdims=True) + eps_norm) * strength) + query_extra[...]
        key = key * lax.rsqrt(jnp.sum(key * key, -1, keepdims=True) + eps_norm) + key_extra[...] * strength
        out[g, 0] = query.astype(jnp.bfloat16)
        out[g, 1] = key.astype(jnp.bfloat16)
        out[g, 2] = (value + ones).astype(jnp.bfloat16)


def attend_kernel(size, places, fast, scales, queries, first, second, out, held):
    head = pl.program_id(0)
    heads, total = held.shape[0], held.shape[1]
    count, piece_rows, _ = out.shape
    halves = (first, second)
    contract = (((1,), (1,)), ((), ()))
    block = math.gcd(total, 256)

    def body(with_max):
        for begin in range(0, total, block):
            query = queries[0, 0, begin : begin + block, :]
            scores = [
                lax.dot_general(query, part[0, 1], contract, preferred_element_type=jnp.float32) for part in halves
            ]
            if with_max:
                strength = scales[head] * math.log2(math.e)
                top = jnp.maximum(jnp.max(scores[0], -1, keepdims=True), jnp.max(scores[1], -1, keepdims=True))
                scores = [(s - top) * strength for s in scores]
            mixed = sum(
                jnp.dot(jnp.exp2(s).astype(jnp.bfloat16), part[0, 2], preferred_element_type=jnp.float32)
                for s, part in zip(scores, halves)
            )
            held[head, begin : begin + block, :] = mixed[:, :size] / mixed[:, size : size + 1]

    @pl.when(fast[0] == 1)
    def _():
        body(False)

    @pl.when(fast[0] == 0)
    def _():
        body(True)

    @pl.when(head == heads - 1)
    def _():
        for j in range(count):
            rows = pl.ds(pl.multiple_of(places[j] * piece_rows, piece_rows), piece_rows)
            out[j] = jnp.concatenate([held[h, rows, :] for h in range(heads)], -1).astype(jnp.bfloat16)


def finish_kernel(count, mixed, ints, places, *refs):
    if mixed:
        tile, left, right = refs[:3]
        refs = refs[3:]
    else:
        tile = refs[0]
        refs = refs[1:]
    pieces, weight, gate, out = refs[:count], refs[count], refs[count + 1], refs[count + 2]
    inner = pieces[0].shape[-1]
    rows, cols, _ = tile.shape
    half = cols // 2
    level, lon = ints[0], ints[2]
    total = 0.0
    for j in range(count):
        begin = pl.multiple_of(places[j] * inner, inner)
        total = total + jnp.dot(pieces[j][...], weight[pl.ds(begin, inner), :], preferred_element_type=jnp.float32)
    branch = gate[pl.ds(level, 1), :] * total.astype(jnp.bfloat16).astype(jnp.float32)
    first = pl.multiple_of(jnp.where(lon > half, 0, half), half)
    for r in range(rows):
        if mixed:
            residual = mixed_half(r, lon, tile, left, right)
        else:
            residual = tile[r, pl.ds(first, half), :].astype(jnp.float32)
        out[r] = (residual + branch[r * half : (r + 1) * half]).astype(jnp.bfloat16)


def shards(
    latents, timesteps, offsets, qkv_weight, logit_scale, out_weight, mod_shift, mod_scale, mod_gate
):
    tile = latents[0]
    rows, cols, width = tile.shape
    half = cols // 2
    heads = qkv_weight.shape[2]
    size = qkv_weight.shape[3] // 3
    inner = heads * size
    n = lax.axis_size("seq")
    me = lax.axis_index("seq")
    masks = [0]
    bits = [1 << i for i in range(n.bit_length() - 1)]
    for bit in reversed(bits):
        masks = masks + [m | bit for m in masks]
    places = jnp.bitwise_xor(me, jnp.asarray(masks, jnp.int32))
    lat, lon = offsets[0, 0], offsets[0, 1]
    ints = jnp.stack([timesteps[0], lat, lon])
    scales = logit_scale[0]
    fast = (jnp.max(scales) <= constant_shift_scale).astype(jnp.int32)[None]
    shift, scale, gate = mod_shift[0], mod_scale[0], mod_gate[0]
    piece_rows = rows * half
    half_tokens = n * piece_rows

    right = passed_along(tile[:, :half], "win", -1)
    left = passed_along(tile[:, half:], "win", 1)

    weight = jnp.transpose(qkv_weight[0], (1, 2, 0))
    group = 2 if heads % 2 == 0 else 1

    def gathered(piece):
        pieces = [piece]
        for bit in reversed(bits):
            pieces = pieces + [swapped(p, "seq", bit) for p in pieces]
        return pieces

    def projected(pieces):
        return pl.pallas_call(
            functools.partial(project_kernel, n, half, size),
            grid=(heads // group,),
            out_shape=jax.ShapeDtypeStruct((heads, 3, half_tokens, lane), jnp.bfloat16),
            in_specs=[SMEM, SMEM, SMEM, SMEM]
            + [pl.BlockSpec((piece_rows, width), lambda h: (0, 0))] * n
            + [pl.BlockSpec((group, 3 * size, width), lambda h: (h, 0, 0))],
            out_specs=pl.BlockSpec((group, 3, half_tokens, lane), lambda h: (h, 0, 0, 0)),
            scratch_shapes=[
                pltpu.VMEM((half_tokens, width), jnp.bfloat16),
                pltpu.VMEM((group * 3 * lane, width), jnp.bfloat16),
                pltpu.VMEM((half_tokens, lane), jnp.float32),
                pltpu.VMEM((half_tokens, lane), jnp.float32),
            ],
            compiler_params=params(),
            cost_estimate=small,
            name="project",
        )(ints, places, fast, scales, *[p.reshape(piece_rows, width) for p in pieces], weight)

    half_shape = jax.ShapeDtypeStruct((rows, half, width), jnp.bfloat16)
    local = pl.pallas_call(
        local_half_kernel,
        out_shape=half_shape,
        in_specs=[SMEM, VMEM, VMEM, VMEM],
        out_specs=VMEM,
        compiler_params=params(),
        cost_estimate=small,
        name="norm_local",
    )(ints, tile, shift, scale)
    local_pieces = gathered(local)
    mixed = pl.pallas_call(
        mixed_half_kernel,
        out_shape=half_shape,
        in_specs=[SMEM, VMEM, VMEM, VMEM, VMEM, VMEM],
        out_specs=VMEM,
        compiler_params=params(),
        cost_estimate=small,
        name="norm_mixed",
    )(ints, tile, left, right, shift, scale)
    mixed_pieces = gathered(mixed)
    local_heads = projected(local_pieces)
    mixed_heads = projected(mixed_pieces)

    def attended(own, first, second):
        whole = pl.BlockSpec((1, 3, half_tokens, lane), lambda h, *_: (h, 0, 0, 0))
        return pl.pallas_call(
            functools.partial(attend_kernel, size),
            grid_spec=pltpu.PrefetchScalarGridSpec(
                num_scalar_prefetch=3,
                grid=(heads,),
                in_specs=[
                    pl.BlockSpec((1, 1, half_tokens, lane), lambda h, *_: (h, 0, 0, 0)),
                    whole,
                    whole,
                ],
                out_specs=pl.BlockSpec((n, piece_rows, inner), lambda h, *_: (0, 0, 0)),
                scratch_shapes=[pltpu.VMEM((heads, half_tokens, size), jnp.float32)],
            ),
            out_shape=jax.ShapeDtypeStruct((n, piece_rows, inner), jnp.bfloat16),
            compiler_params=params(),
            cost_estimate=small,
            name="attend",
        )(places, fast, scales, own, first, second)

    def hop(held, bit):
        middle = held.shape[1] // 2
        return held[:, :middle], swapped(held[:, middle:], "seq", bit)

    def returned(held):
        held = jnp.concatenate(held, 0)
        for bit in bits[1:]:
            held = jnp.concatenate(hop(held, bit), 0)
        return [held[g, 0] for g in range(n)]

    order = [0]
    for bit in bits:
        order = order + [m | bit for m in order]
    sources = jnp.bitwise_xor(me, jnp.asarray(order, jnp.int32))

    def finished(groups, extra, is_mixed):
        block = width // 3 if width % (3 * lane) == 0 else width
        sides = pl.BlockSpec((rows, half, block), lambda i: (0, 0, i))
        return pl.pallas_call(
            functools.partial(finish_kernel, n, is_mixed),
            grid=(width // block,),
            out_shape=half_shape,
            in_specs=[SMEM, SMEM, pl.BlockSpec((rows, cols, block), lambda i: (0, 0, i))]
            + [sides] * len(extra)
            + [pl.BlockSpec((piece_rows, inner), lambda i: (0, 0))] * n
            + [pl.BlockSpec((width, block), lambda i: (0, i)), pl.BlockSpec((gate.shape[0], block), lambda i: (0, i))],
            out_specs=sides,
            compiler_params=params(),
            cost_estimate=small,
            name="finish",
        )(ints, sources, tile, *extra, *groups, out_weight[0], gate)

    mixed_kept, mixed_received = hop(attended(mixed_heads, local_heads, mixed_heads)[None], bits[0])
    local_query, mixed_received = lax.optimization_barrier((local_heads, mixed_received))
    mixed_out = returned((mixed_kept, mixed_received))
    local_out = returned(hop(attended(local_query, local_query, mixed_heads)[None], bits[0]))
    mixed_done = finished(mixed_out, [left, right], True)
    up = passed_along(mixed_done, "win", 1)
    down = passed_along(mixed_done, "win", -1)
    local_done = finished(local_out, [], False)
    local_sent = passed_along(local_done, "segment", 1)
    big = lon > half
    column = lax.iota(jnp.int32, half) + jnp.where(big, half, 0)
    far_side = jnp.where(big, column >= lon, column < lon)
    mixed_back = jnp.where(far_side[None, :, None], jnp.where(big, down, up), mixed_done)
    mixed_sent = passed_along(mixed_back, "segment", 1)
    source_lon = passed_along(offsets, "segment", 1)[0, 1]
    source_big = source_lon > half
    low = jnp.where(source_big, local_sent, mixed_sent)
    high = jnp.where(source_big, mixed_sent, local_sent)
    return jnp.concatenate([low, high], axis=1)[None]


def solution(mesh):
    in_specs = (
        P("segment", "seq", "win", None),
        P("segment"),
        P("segment", None),
        P("segment", None, "seq", None),
        P("segment", "seq"),
        P("segment", None, None),
        P("segment", None, None),
        P("segment", None, None),
        P("segment", None, None),
    )
    out_specs = P("segment", "seq", "win", None)
    return jax.shard_map(shards, mesh=mesh, in_specs=in_specs, out_specs=out_specs, check_vma=False)
```

```python
import functools
import math

import jax
import jax.numpy as jnp
from jax import lax
from jax.experimental import pallas as pl
from jax.experimental.pallas import tpu as pltpu
from jax.sharding import PartitionSpec as P

eps_norm = 1e-06
lane = 128
far = 1e30
constant_shift_scale = 32.0

SMEM = pl.BlockSpec(memory_space=pltpu.SMEM)
VMEM = pl.BlockSpec(memory_space=pltpu.VMEM)


small = pl.CostEstimate(flops=1, bytes_accessed=1, transcendentals=0)


def params(mib=40):
    return pltpu.CompilerParams(vmem_limit_bytes=mib << 20)


def passed_along(block, axis, distance):
    n = lax.axis_size(axis)
    return lax.ppermute(block, axis, [(i, (i + distance) % n) for i in range(n)])


def swapped(block, axis, mask):
    return lax.ppermute(block, axis, [(i, i ^ mask) for i in range(lax.axis_size(axis))])


def places_of(masks):
    me = lax.axis_index("seq")
    return [me ^ m for m in masks]


def all_gentle(scales):
    top = scales[0, 0]
    for h in range(1, scales.shape[1]):
        top = jnp.maximum(top, scales[0, h])
    return top <= constant_shift_scale


def normalise(x, scale_row, shift_row):
    x = x - jnp.mean(x, -1, keepdims=True)
    variance = jnp.mean(x * x, -1, keepdims=True)
    return (x * lax.rsqrt(variance + eps_norm) * scale_row + shift_row).astype(jnp.bfloat16)


def local_half_kernel(level, offsets, tile, shift, scale, out):
    row = pl.ds(level[0] % shift.shape[0], 1)
    for r in range(tile.shape[0]):
        out[r] = normalise(tile[r].astype(jnp.float32), scale[row, :], shift[row, :])


def mixed_half(r, lon, half, tile, borrowed):
    big = lon > half
    column = lax.broadcasted_iota(jnp.int32, (half, 1), 0) + jnp.where(big, half, 0)
    far_side = jnp.where(big, (column >= lon).astype(jnp.int32), (column < lon).astype(jnp.int32)) == 1
    return jnp.where(far_side, borrowed[r].astype(jnp.float32), tile[r].astype(jnp.float32))


def mixed_half_kernel(level, offsets, tile, borrowed, shift, scale, out):
    row = pl.ds(level[0] % shift.shape[0], 1)
    for r in range(tile.shape[0]):
        x = mixed_half(r, offsets[0, 1], tile.shape[1], tile, borrowed)
        out[r] = normalise(x, scale[row, :], shift[row, :])


def project_kernel(masks, half, size, offsets, scales, *refs):
    count = len(masks)
    places = places_of(masks)
    pieces, weight, out = refs[:count], refs[count], refs[count + 1]
    tokens, padded, query_extra, key_extra = refs[count + 2 :]
    piece_rows = pieces[0].shape[0]
    group = weight.shape[0]
    total = tokens.shape[0]
    step = pl.program_id(0)

    @pl.when(step == 0)
    def _():
        padded[...] = jnp.zeros_like(padded)
        for j in range(count):
            tokens[pl.ds(pl.multiple_of(places[j] * piece_rows, piece_rows), piece_rows), :] = pieces[j][...]
        row = lax.broadcasted_iota(jnp.int32, (total, lane), 0) // half
        column = lax.broadcasted_iota(jnp.int32, (total, lane), 1)
        low = jnp.where(row < offsets[0, 0], 1.0, 0.0)
        query_extra[...] = jnp.where(
            column == size, low, jnp.where(column == size + 1, 1.0 - low, jnp.where(column == size + 2, 1.0, 0.0))
        )
        key_extra[...] = jnp.where(
            column == size,
            far * (low - 1.0),
            jnp.where(column == size + 1, -far * low, jnp.where(column == size + 2, -1.0, 0.0)),
        )

    for g in range(group):
        for i in range(3):
            begin = (3 * g + i) * lane
            padded[begin : begin + size, :] = weight[g, i * size : (i + 1) * size, :]
    mixture = lax.dot_general(
        tokens[...], padded[...], (((1,), (1,)), ((), ())), preferred_element_type=jnp.float32
    )
    ones = jnp.where(lax.broadcasted_iota(jnp.int32, (1, lane), 1) == size, 1.0, 0.0)
    fast = all_gentle(scales)
    for g in range(group):
        strength = jnp.where(fast, scales[0, step * group + g] * math.log2(math.e), 1.0)
        query, key, value = (mixture[:, (3 * g + i) * lane : (3 * g + i + 1) * lane] for i in range(3))
        query = query * (lax.rsqrt(jnp.sum(query * query, -1, keepdims=True) + eps_norm) * strength) + query_extra[...]
        key = key * lax.rsqrt(jnp.sum(key * key, -1, keepdims=True) + eps_norm) + key_extra[...] * strength
        out[g, 0] = query.astype(jnp.bfloat16)
        out[g, 1] = key.astype(jnp.bfloat16)
        out[g, 2] = (value + ones).astype(jnp.bfloat16)


def attend_kernel(masks, size, scales, queries, first, second, out, held):
    places = places_of(masks)
    fast = all_gentle(scales)
    head = pl.program_id(0)
    heads, total = held.shape[0], held.shape[1]
    count, piece_rows, _ = out.shape
    halves = (first, second)
    contract = (((1,), (1,)), ((), ()))
    block = math.gcd(total, 256)

    def body(with_max):
        for begin in range(0, total, block):
            query = queries[0, 0, begin : begin + block, :]
            scores = [
                lax.dot_general(query, part[0, 1], contract, preferred_element_type=jnp.float32) for part in halves
            ]
            if with_max:
                strength = scales[0, head] * math.log2(math.e)
                top = jnp.maximum(jnp.max(scores[0], -1, keepdims=True), jnp.max(scores[1], -1, keepdims=True))
                scores = [(s - top) * strength for s in scores]
            mixed = sum(
                jnp.dot(jnp.exp2(s).astype(jnp.bfloat16), part[0, 2], preferred_element_type=jnp.float32)
                for s, part in zip(scores, halves)
            )
            held[head, begin : begin + block, :] = mixed[:, :size] / mixed[:, size : size + 1]

    @pl.when(fast)
    def _():
        body(False)

    @pl.when(jnp.logical_not(fast))
    def _():
        body(True)

    @pl.when(head == heads - 1)
    def _():
        for j in range(count):
            rows = pl.ds(pl.multiple_of(places[j] * piece_rows, piece_rows), piece_rows)
            out[j] = jnp.concatenate([held[h, rows, :] for h in range(heads)], -1).astype(jnp.bfloat16)


def finish_kernel(masks, mixed, level, offsets, tile, *refs):
    count = len(masks)
    places = places_of(masks)
    if mixed:
        borrowed, refs = refs[0], refs[1:]
    pieces, weight, gate, out = refs[:count], refs[count], refs[count + 1], refs[count + 2]
    inner = pieces[0].shape[-1]
    rows, half, _ = tile.shape
    total = 0.0
    for j in range(count):
        begin = pl.multiple_of(places[j] * inner, inner)
        total = total + jnp.dot(pieces[j][...], weight[pl.ds(begin, inner), :], preferred_element_type=jnp.float32)
    branch = gate[pl.ds(level[0] % gate.shape[0], 1), :] * total.astype(jnp.bfloat16).astype(jnp.float32)
    for r in range(rows):
        if mixed:
            residual = mixed_half(r, offsets[0, 1], half, tile, borrowed)
        else:
            residual = tile[r].astype(jnp.float32)
        out[r] = (residual + branch[r * half : (r + 1) * half]).astype(jnp.bfloat16)


def assemble_kernel(source_offsets, local, mixed, out):
    half = local.shape[1]
    big = source_offsets[0, 1] > half
    first = pl.multiple_of(jnp.where(big, 0, half), half)
    second = pl.multiple_of(jnp.where(big, half, 0), half)
    out[0, :, pl.ds(first, half), :] = local[...]
    out[0, :, pl.ds(second, half), :] = mixed[...]


def shards(
    latents, timesteps, offsets, qkv_weight, logit_scale, out_weight, mod_shift, mod_scale, mod_gate
):
    tile = latents[0]
    rows, cols, width = tile.shape
    half = cols // 2
    heads = qkv_weight.shape[2]
    size = qkv_weight.shape[3] // 3
    inner = heads * size
    n = lax.axis_size("seq")
    masks = [0]
    bits = [1 << i for i in range(n.bit_length() - 1)]
    for bit in reversed(bits):
        masks = masks + [m | bit for m in masks]
    shift, scale, gate = mod_shift[0], mod_scale[0], mod_gate[0]
    piece_rows = rows * half
    half_tokens = n * piece_rows

    weight = jnp.transpose(qkv_weight[0], (1, 2, 0))
    group = 2 if heads % 2 == 0 else 1

    source_offsets = passed_along(offsets, "segment", 1)
    lon = offsets[0, 1]
    big = lon > half

    def gathered(pieces):
        for bit in reversed(bits[:-1]):
            pieces = pieces + [swapped(p, "seq", bit) for p in pieces]
        return pieces

    def projected(pieces):
        return pl.pallas_call(
            functools.partial(project_kernel, masks, half, size),
            grid=(heads // group,),
            out_shape=jax.ShapeDtypeStruct((heads, 3, half_tokens, lane), jnp.bfloat16),
            in_specs=[SMEM, SMEM]
            + [pl.BlockSpec((piece_rows, width), lambda h: (0, 0))] * n
            + [pl.BlockSpec((group, 3 * size, width), lambda h: (h, 0, 0))],
            out_specs=pl.BlockSpec((group, 3, half_tokens, lane), lambda h: (h, 0, 0, 0)),
            scratch_shapes=[
                pltpu.VMEM((half_tokens, width), jnp.bfloat16),
                pltpu.VMEM((group * 3 * lane, width), jnp.bfloat16),
                pltpu.VMEM((half_tokens, lane), jnp.float32),
                pltpu.VMEM((half_tokens, lane), jnp.float32),
            ],
            compiler_params=params(),
            cost_estimate=small,
            name="project",
        )(offsets, logit_scale, *[p.reshape(piece_rows, width) for p in pieces], weight)

    half_shape = jax.ShapeDtypeStruct((rows, half, width), jnp.bfloat16)
    def is_big(offsets):
        return (offsets[0, 1] > half).astype(jnp.int32)

    def normed(kernel, name, low_if_big, *arrays):
        block = math.gcd(rows, 4)
        table = math.gcd(shift.shape[0], 8)

        def own(i, level, offsets):
            return i, is_big(offsets) ^ low_if_big, 0

        return pl.pallas_call(
            kernel,
            grid_spec=pltpu.PrefetchScalarGridSpec(
                num_scalar_prefetch=2,
                grid=(rows // block,),
                in_specs=[pl.BlockSpec((block, half, width), own)]
                + [pl.BlockSpec((block, half, width), lambda i, *_: (i, 0, 0))] * (len(arrays) - 1)
                + [pl.BlockSpec((table, width), lambda i, level, offsets: (level[0] // table, 0))] * 2,
                out_specs=pl.BlockSpec((block, half, width), lambda i, *_: (i, 0, 0)),
            ),
            out_shape=half_shape,
            compiler_params=params(),
            cost_estimate=small,
            name=name,
        )(timesteps, offsets, *arrays, shift, scale)

    def window_heads(borrowed):
        local = normed(local_half_kernel, "norm_local", 1, tile)
        local_far = swapped(local, "seq", bits[-1])
        mixed = normed(mixed_half_kernel, "norm_mixed", 0, tile, *borrowed)
        local_far, mixed = lax.optimization_barrier((local_far, mixed))
        local_heads = projected(gathered([local, local_far]))
        mixed_far = swapped(mixed, "seq", bits[-1])
        mixed_far, local_heads = lax.optimization_barrier((mixed_far, local_heads))
        return local_heads, projected(gathered([mixed, mixed_far])), borrowed

    def from_next(tile):
        return window_heads([passed_along(tile[:, :half], "win", -1)])

    def from_before(tile):
        return window_heads([passed_along(tile[:, half:], "win", 1)])

    local_heads, mixed_heads, borrowed = lax.cond(big, from_before, from_next, tile)
    local_heads, source_offsets = lax.optimization_barrier((local_heads, source_offsets))

    def attended(own, first, second):
        whole = pl.BlockSpec((1, 3, half_tokens, lane), lambda h: (h, 0, 0, 0))
        return pl.pallas_call(
            functools.partial(attend_kernel, masks, size),
            grid=(heads,),
            in_specs=[SMEM, pl.BlockSpec((1, 1, half_tokens, lane), lambda h: (h, 0, 0, 0)), whole, whole],
            out_specs=pl.BlockSpec((n, piece_rows, inner), lambda h: (0, 0, 0)),
            scratch_shapes=[pltpu.VMEM((heads, half_tokens, size), jnp.float32)],
            out_shape=jax.ShapeDtypeStruct((n, piece_rows, inner), jnp.bfloat16),
            compiler_params=params(),
            cost_estimate=small,
            name="attend",
        )(logit_scale, own, first, second)

    def hop(held, bit):
        middle = held.shape[1] // 2
        return held[:, :middle], swapped(held[:, middle:], "seq", bit)

    def returned(held):
        held = jnp.concatenate(held, 0)
        for bit in bits[1:]:
            held = jnp.concatenate(hop(held, bit), 0)
        return [held[g, 0] for g in range(n)]

    order = [0]
    for bit in bits:
        order = order + [m | bit for m in order]

    def finished(groups, extra, is_mixed):
        block = width // 3 if width % (3 * lane) == 0 else width
        table = math.gcd(gate.shape[0], 8)
        sides = pl.BlockSpec((rows, half, block), lambda i, *_: (0, 0, i))
        low_if_big = 0 if is_mixed else 1
        return pl.pallas_call(
            functools.partial(finish_kernel, order, is_mixed),
            grid_spec=pltpu.PrefetchScalarGridSpec(
                num_scalar_prefetch=2,
                grid=(width // block,),
                in_specs=[
                    pl.BlockSpec(
                        (rows, half, block), lambda i, level, offsets: (0, is_big(offsets) ^ low_if_big, i)
                    )
                ]
                + [sides] * len(extra)
                + [pl.BlockSpec((piece_rows, inner), lambda i, *_: (0, 0))] * n
                + [
                    pl.BlockSpec((width, block), lambda i, *_: (0, i)),
                    pl.BlockSpec((table, block), lambda i, level, offsets: (level[0] // table, i)),
                ],
                out_specs=sides,
            ),
            out_shape=half_shape,
            compiler_params=params(),
            cost_estimate=small,
            name="finish",
        )(timesteps, offsets, tile, *extra, *groups, out_weight[0], gate)

    mixed_kept, mixed_received = hop(attended(mixed_heads, local_heads, mixed_heads)[None], bits[0])
    local_query, mixed_received = lax.optimization_barrier((local_heads, mixed_received))
    mixed_out = returned((mixed_kept, mixed_received))
    local_out = returned(hop(attended(local_query, local_query, mixed_heads)[None], bits[0]))
    mixed_done = finished(mixed_out, borrowed, True)
    up = passed_along(mixed_done, "win", 1)
    down = passed_along(mixed_done, "win", -1)
    local_done = finished(local_out, [], False)
    local_sent = passed_along(local_done, "segment", 1)
    column = lax.iota(jnp.int32, half) + jnp.where(big, half, 0)
    far_side = jnp.where(big, column >= lon, column < lon)
    mixed_back = jnp.where(far_side[None, :, None], jnp.where(big, down, up), mixed_done)
    mixed_sent = passed_along(mixed_back, "segment", 1)
    return pl.pallas_call(
        assemble_kernel,
        out_shape=jax.ShapeDtypeStruct((1, rows, cols, width), jnp.bfloat16),
        in_specs=[SMEM, VMEM, VMEM],
        out_specs=VMEM,
        compiler_params=params(),
        cost_estimate=small,
        name="assemble",
    )(source_offsets, local_sent, mixed_sent)


def solution(mesh):
    in_specs = (
        P("segment", "seq", "win", None),
        P("segment"),
        P("segment", None),
        P("segment", None, "seq", None),
        P("segment", "seq"),
        P("segment", None, None),
        P("segment", None, None),
        P("segment", None, None),
        P("segment", None, None),
    )
    out_specs = P("segment", "seq", "win", None)
    return jax.shard_map(shards, mesh=mesh, in_specs=in_specs, out_specs=out_specs, check_vma=False)
```

```python
import functools
import math

import jax
import jax.numpy as jnp
from jax import lax
from jax.experimental import pallas as pl
from jax.experimental.pallas import tpu as pltpu
from jax.sharding import PartitionSpec as P

eps_norm = 1e-06
lane = 128
far = 1e30
constant_shift_scale = 32.0

SMEM = pl.BlockSpec(memory_space=pltpu.SMEM)
VMEM = pl.BlockSpec(memory_space=pltpu.VMEM)


small = pl.CostEstimate(flops=1, bytes_accessed=1, transcendentals=0)


def params(mib=40):
    return pltpu.CompilerParams(vmem_limit_bytes=mib << 20)


def passed_along(block, axis, distance):
    n = lax.axis_size(axis)
    return lax.ppermute(block, axis, [(i, (i + distance) % n) for i in range(n)])


def swapped(block, axis, mask):
    return lax.ppermute(block, axis, [(i, i ^ mask) for i in range(lax.axis_size(axis))])


def places_of(masks):
    me = lax.axis_index("seq")
    return [me ^ m for m in masks]


def gathered_masks(held, bits):
    for bit in reversed(bits[:-1]):
        held = held + [m | bit for m in held]
    return held


def all_gentle(scales):
    top = scales[0, 0]
    for h in range(1, scales.shape[1]):
        top = jnp.maximum(top, scales[0, h])
    return top <= constant_shift_scale


def normalise(x, scale_row, shift_row):
    x = x - jnp.mean(x, -1, keepdims=True)
    variance = jnp.mean(x * x, -1, keepdims=True)
    return (x * lax.rsqrt(variance + eps_norm) * scale_row + shift_row).astype(jnp.bfloat16)


def project_kernel(masks, rows, size, level, offsets, scales, *refs):
    count = len(masks)
    places = places_of(masks)
    pieces = refs[:count]
    weight, shift, scale, out, tokens, padded, query_extra, key_extra = refs[count:]
    piece_rows = pieces[0].shape[0]
    half = piece_rows // rows
    group = weight.shape[0]
    step = pl.program_id(0)

    @pl.when(step == 0)
    def _():
        padded[...] = jnp.zeros_like(padded)
        shift_row, scale_row = shift[pl.ds(level[0], 1), :], scale[pl.ds(level[0], 1), :]
        column = lax.broadcasted_iota(jnp.int32, (piece_rows, lane), 1)
        local_row = lax.broadcasted_iota(jnp.int32, (piece_rows, lane), 0) // half
        chunk = math.gcd(piece_rows, 32)
        for j in range(count):
            for begin in range(0, piece_rows, chunk):
                x = pieces[j][begin : begin + chunk, :].astype(jnp.float32)
                at = j * piece_rows + begin
                tokens[at : at + chunk, :] = normalise(x, scale_row, shift_row)
            low = jnp.where(local_row + places[j] * rows < offsets[0, 0], 1.0, 0.0)
            span = slice(j * piece_rows, (j + 1) * piece_rows)
            query_extra[span, :] = jnp.where(
                column == size, low, jnp.where(column == size + 1, 1.0 - low, jnp.where(column == size + 2, 1.0, 0.0))
            )
            key_extra[span, :] = jnp.where(
                column == size,
                far * (low - 1.0),
                jnp.where(column == size + 1, -far * low, jnp.where(column == size + 2, -1.0, 0.0)),
            )

    for g in range(group):
        for i in range(3):
            begin = (3 * g + i) * lane
            padded[begin : begin + size, :] = weight[g, i * size : (i + 1) * size, :]
    mixture = lax.dot_general(
        tokens[...], padded[...], (((1,), (1,)), ((), ())), preferred_element_type=jnp.float32
    )
    ones = jnp.where(lax.broadcasted_iota(jnp.int32, (1, lane), 1) == size, 1.0, 0.0)
    fast = all_gentle(scales)
    for g in range(group):
        strength = jnp.where(fast, scales[0, step * group + g] * math.log2(math.e), 1.0)
        query, key, value = (mixture[:, (3 * g + i) * lane : (3 * g + i + 1) * lane] for i in range(3))
        query = query * (lax.rsqrt(jnp.sum(query * query, -1, keepdims=True) + eps_norm) * strength) + query_extra[...]
        key = key * lax.rsqrt(jnp.sum(key * key, -1, keepdims=True) + eps_norm) + key_extra[...] * strength
        out[g, 0] = query.astype(jnp.bfloat16)
        out[g, 1] = key.astype(jnp.bfloat16)
        out[g, 2] = (value + ones).astype(jnp.bfloat16)


def attend_kernel(own_count, own_masks, out_masks, size, scales, *refs):
    queries, parts, out, held = refs[:own_count], refs[own_count:-2], refs[-2], refs[-1]
    fast = all_gentle(scales)
    head = pl.program_id(0)
    heads = held.shape[0]
    piece_rows = out.shape[1]
    contract = (((1,), (1,)), ((), ()))

    def body(with_max):
        at = 0
        for own in queries:
            block = math.gcd(own.shape[2], 256)
            for begin in range(0, own.shape[2], block):
                query = own[0, 0, begin : begin + block, :]
                scores = [
                    lax.dot_general(query, part[0, 1], contract, preferred_element_type=jnp.float32) for part in parts
                ]
                if with_max:
                    strength = scales[0, head] * math.log2(math.e)
                    top = functools.reduce(jnp.maximum, [jnp.max(s, -1, keepdims=True) for s in scores])
                    scores = [(s - top) * strength for s in scores]
                mixed = sum(
                    jnp.dot(jnp.exp2(s).astype(jnp.bfloat16), part[0, 2], preferred_element_type=jnp.float32)
                    for s, part in zip(scores, parts)
                )
                held[head, at : at + block, :] = mixed[:, :size] / mixed[:, size : size + 1]
                at += block

    @pl.when(fast)
    def _():
        body(False)

    @pl.when(jnp.logical_not(fast))
    def _():
        body(True)

    @pl.when(head == heads - 1)
    def _():
        for j, mask in enumerate(out_masks):
            begin = own_masks.index(mask) * piece_rows
            out[j] = jnp.concatenate(
                [held[h, begin : begin + piece_rows, :] for h in range(heads)], -1
            ).astype(jnp.bfloat16)


def finish_kernel(masks, level, tile, *refs):
    count = len(masks)
    places = places_of(masks)
    pieces, weight, gate, out = refs[:count], refs[count], refs[count + 1], refs[count + 2]
    inner = pieces[0].shape[-1]
    rows, half, _ = tile.shape
    total = 0.0
    for j in range(count):
        begin = pl.multiple_of(places[j] * inner, inner)
        total = total + jnp.dot(pieces[j][...], weight[pl.ds(begin, inner), :], preferred_element_type=jnp.float32)
    branch = gate[pl.ds(level[0], 1), :] * total.astype(jnp.bfloat16).astype(jnp.float32)
    for r in range(rows):
        out[r] = (tile[r].astype(jnp.float32) + branch[r * half : (r + 1) * half]).astype(jnp.bfloat16)


def assemble_kernel(offsets, local, mixed, moved, out):
    rows, half, _ = local.shape
    lon = offsets[0, 1]
    big = lon > half
    first = pl.multiple_of(jnp.where(big, 0, half), half)
    second = pl.multiple_of(jnp.where(big, half, 0), half)
    column = lax.broadcasted_iota(jnp.int32, (half, 1), 0) + second
    far_side = jnp.where(big, (column >= lon).astype(jnp.int32), (column < lon).astype(jnp.int32)) == 1
    out[0, :, pl.ds(first, half), :] = local[...]
    for r in range(rows):
        out[0, r, pl.ds(second, half), :] = jnp.where(
            far_side, moved[r].astype(jnp.float32), mixed[r].astype(jnp.float32)
        ).astype(jnp.bfloat16)


def shards(
    latents, timesteps, offsets, qkv_weight, logit_scale, out_weight, mod_shift, mod_scale, mod_gate
):
    tile = latents[0]
    rows, cols, width = tile.shape
    half = cols // 2
    heads = qkv_weight.shape[2]
    size = qkv_weight.shape[3] // 3
    inner = heads * size
    n = lax.axis_size("seq")
    masks = [0]
    bits = [1 << i for i in range(n.bit_length() - 1)]
    for bit in reversed(bits):
        masks = masks + [m | bit for m in masks]
    shift, scale, gate = mod_shift[0], mod_scale[0], mod_gate[0]
    piece_rows = rows * half
    half_tokens = n * piece_rows

    weight = jnp.transpose(qkv_weight[0], (1, 2, 0))
    group = 2 if heads % 2 == 0 else 1

    source_offsets = passed_along(offsets, "segment", 1)
    lon = offsets[0, 1]
    big = lon > half

    half_shape = jax.ShapeDtypeStruct((rows, half, width), jnp.bfloat16)

    def gathered(pieces):
        for bit in reversed(bits[:-1]):
            pieces = pieces + [swapped(p, "seq", bit) for p in pieces]
        return pieces

    def projected(pieces, held_masks):
        tokens = len(pieces) * piece_rows
        table = pl.BlockSpec(shift.shape, lambda h: (0, 0))
        return pl.pallas_call(
            functools.partial(project_kernel, held_masks, rows, size),
            grid=(heads // group,),
            out_shape=jax.ShapeDtypeStruct((heads, 3, tokens, lane), jnp.bfloat16),
            in_specs=[SMEM, SMEM, SMEM]
            + [pl.BlockSpec((piece_rows, width), lambda h: (0, 0))] * len(pieces)
            + [pl.BlockSpec((group, 3 * size, width), lambda h: (h, 0, 0)), table, table],
            out_specs=pl.BlockSpec((group, 3, tokens, lane), lambda h: (h, 0, 0, 0)),
            scratch_shapes=[
                pltpu.VMEM((tokens, width), jnp.bfloat16),
                pltpu.VMEM((group * 3 * lane, width), jnp.bfloat16),
                pltpu.VMEM((tokens, lane), jnp.float32),
                pltpu.VMEM((tokens, lane), jnp.float32),
            ],
            compiler_params=params(),
            cost_estimate=small,
            name="project",
        )(timesteps, offsets, logit_scale, *[p.reshape(piece_rows, width) for p in pieces], weight, shift, scale)

    top = bits[-1]
    local_masks = gathered_masks([0, top], bits)
    near_masks = gathered_masks([0], bits)
    far_masks = [m | top for m in near_masks]

    low, high = tile[:, :half], tile[:, half:]
    local = jnp.where(big, low, high)
    local_far = swapped(local, "seq", top)

    def mixed_half(from_before, tile, lon):
        low, high = tile[:, :half], tile[:, half:]
        own = high if from_before else low
        borrowed = passed_along(own, "win", 1 if from_before else -1)
        column = lax.broadcasted_iota(jnp.int32, own.shape, 1)
        return jnp.where(column + half >= lon if from_before else column < lon, borrowed, own)

    mixed = lax.cond(big, functools.partial(mixed_half, True), functools.partial(mixed_half, False), tile, lon)
    local_far, mixed = lax.optimization_barrier((local_far, mixed))
    local_heads = projected(gathered([local, local_far]), local_masks)
    mixed_far = swapped(mixed, "seq", top)
    near_heads = projected(gathered([mixed]), near_masks)
    mixed_far, local_heads, near_heads, source_offsets = lax.optimization_barrier(
        (mixed_far, local_heads, near_heads, source_offsets)
    )
    far_heads = projected(gathered([mixed_far]), far_masks)

    def attended(own, own_masks, local_heads):
        def block(array, kinds):
            return pl.BlockSpec((1, kinds, array.shape[2], lane), lambda h: (h, 0, 0, 0))

        parts = [local_heads, near_heads, far_heads]
        total = sum(o.shape[2] for o in own)
        return pl.pallas_call(
            functools.partial(attend_kernel, len(own), own_masks, masks, size),
            grid=(heads,),
            in_specs=[SMEM] + [block(o, 1) for o in own] + [block(p, 3) for p in parts],
            out_specs=pl.BlockSpec((n, piece_rows, inner), lambda h: (0, 0, 0)),
            scratch_shapes=[pltpu.VMEM((heads, total, size), jnp.float32)],
            out_shape=jax.ShapeDtypeStruct((n, piece_rows, inner), jnp.bfloat16),
            compiler_params=params(),
            cost_estimate=small,
            name="attend",
        )(logit_scale, *own, *parts)

    def hop(held, bit):
        middle = held.shape[1] // 2
        return held[:, :middle], swapped(held[:, middle:], "seq", bit)

    def returned(held):
        held = jnp.concatenate(held, 0)
        for bit in bits[1:]:
            held = jnp.concatenate(hop(held, bit), 0)
        return [held[g, 0] for g in range(n)]

    order = [0]
    for bit in bits:
        order = order + [m | bit for m in order]

    def finished(groups, residual):
        block = width // 3 if width % (3 * lane) == 0 else width
        sides = pl.BlockSpec((rows, half, block), lambda i: (0, 0, i))
        return pl.pallas_call(
            functools.partial(finish_kernel, order),
            grid=(width // block,),
            in_specs=[SMEM, sides]
            + [pl.BlockSpec((piece_rows, inner), lambda i: (0, 0))] * n
            + [pl.BlockSpec((width, block), lambda i: (0, i)), pl.BlockSpec((gate.shape[0], block), lambda i: (0, i))],
            out_specs=sides,
            out_shape=half_shape,
            compiler_params=params(),
            cost_estimate=small,
            name="finish",
        )(timesteps, residual, *groups, out_weight[0], gate)

    mixed_kept, mixed_received = hop(attended([near_heads, far_heads], near_masks + far_masks, local_heads)[None], bits[0])
    local_query, mixed_received = lax.optimization_barrier((local_heads, mixed_received))
    mixed_out = returned((mixed_kept, mixed_received))
    local_kept, local_received = hop(attended([local_query], local_masks, local_query)[None], bits[0])
    mixed_done, local_received = lax.optimization_barrier((finished(mixed_out, mixed), local_received))
    mixed_sent = passed_along(mixed_done, "segment", 1)
    local_done = finished(returned((local_kept, local_received)), local)
    local_sent = passed_along(local_done, "segment", 1)
    mixed_sent, _ = lax.optimization_barrier((mixed_sent, local_done))
    moved = lax.cond(
        source_offsets[0, 1] > half,
        lambda block: passed_along(block, "win", -1),
        lambda block: passed_along(block, "win", 1),
        mixed_sent,
    )
    return pl.pallas_call(
        assemble_kernel,
        out_shape=jax.ShapeDtypeStruct((1, rows, cols, width), jnp.bfloat16),
        in_specs=[SMEM, VMEM, VMEM, VMEM],
        out_specs=VMEM,
        compiler_params=params(),
        cost_estimate=small,
        name="assemble",
    )(source_offsets, local_sent, mixed_sent, moved)


def solution(mesh):
    in_specs = (
        P("segment", "seq", "win", None),
        P("segment"),
        P("segment", None),
        P("segment", None, "seq", None),
        P("segment", "seq"),
        P("segment", None, None),
        P("segment", None, None),
        P("segment", None, None),
        P("segment", None, None),
    )
    out_specs = P("segment", "seq", "win", None)
    return jax.shard_map(shards, mesh=mesh, in_specs=in_specs, out_specs=out_specs, check_vma=False)
```

```python
import functools
import math

import jax
import jax.numpy as jnp
from jax import lax
from jax.experimental import pallas as pl
from jax.experimental.pallas import tpu as pltpu
from jax.sharding import PartitionSpec as P

eps_norm = 1e-06
lane = 128
far = 1e30
constant_shift_scale = 32.0

SMEM = pl.BlockSpec(memory_space=pltpu.SMEM)
VMEM = pl.BlockSpec(memory_space=pltpu.VMEM)


small = pl.CostEstimate(flops=1, bytes_accessed=1, transcendentals=0)


def params(mib=40):
    return pltpu.CompilerParams(vmem_limit_bytes=mib << 20)


def passed_along(block, axis, distance):
    n = lax.axis_size(axis)
    return lax.ppermute(block, axis, [(i, (i + distance) % n) for i in range(n)])


def swapped(block, axis, mask):
    return lax.ppermute(block, axis, [(i, i ^ mask) for i in range(lax.axis_size(axis))])


def places_of(masks):
    me = lax.axis_index("seq")
    return [me ^ m for m in masks]


def gathered_masks(held, bits):
    for bit in reversed(bits[:-1]):
        held = held + [m | bit for m in held]
    return held


def all_gentle(scales):
    top = scales[0, 0]
    for h in range(1, scales.shape[1]):
        top = jnp.maximum(top, scales[0, h])
    return top <= constant_shift_scale


def normalise(x, scale_row, shift_row):
    x = x - jnp.mean(x, -1, keepdims=True)
    variance = jnp.mean(x * x, -1, keepdims=True)
    return (x * lax.rsqrt(variance + eps_norm) * scale_row + shift_row).astype(jnp.bfloat16)


def project_kernel(masks, rows, size, offsets, scales, *refs):
    count = len(masks)
    places = places_of(masks)
    pieces = refs[:count]
    weight, rows_ref, out, tokens, padded, query_extra, key_extra = refs[count:]
    piece_rows = pieces[0].shape[0]
    half = piece_rows // rows
    group = weight.shape[0]
    step = pl.program_id(0)

    @pl.when(step == 0)
    def _():
        padded[...] = jnp.zeros_like(padded)
        shift_row, scale_row = rows_ref[0:1, :], rows_ref[1:2, :]
        column = lax.broadcasted_iota(jnp.int32, (piece_rows, lane), 1)
        local_row = lax.broadcasted_iota(jnp.int32, (piece_rows, lane), 0) // half
        chunk = math.gcd(piece_rows, 32)
        for j in range(count):
            for begin in range(0, piece_rows, chunk):
                x = pieces[j][begin : begin + chunk, :].astype(jnp.float32)
                at = j * piece_rows + begin
                tokens[at : at + chunk, :] = normalise(x, scale_row, shift_row)
            low = jnp.where(local_row + places[j] * rows < offsets[0, 0], 1.0, 0.0)
            span = slice(j * piece_rows, (j + 1) * piece_rows)
            query_extra[span, :] = jnp.where(
                column == size, low, jnp.where(column == size + 1, 1.0 - low, jnp.where(column == size + 2, 1.0, 0.0))
            )
            key_extra[span, :] = jnp.where(
                column == size,
                far * (low - 1.0),
                jnp.where(column == size + 1, -far * low, jnp.where(column == size + 2, -1.0, 0.0)),
            )

    for g in range(group):
        for i in range(3):
            begin = (3 * g + i) * lane
            padded[begin : begin + size, :] = weight[g, i * size : (i + 1) * size, :]
    mixture = lax.dot_general(
        tokens[...], padded[...], (((1,), (1,)), ((), ())), preferred_element_type=jnp.float32
    )
    ones = jnp.where(lax.broadcasted_iota(jnp.int32, (1, lane), 1) == size, 1.0, 0.0)
    fast = all_gentle(scales)
    for g in range(group):
        strength = jnp.where(fast, scales[0, step * group + g] * math.log2(math.e), 1.0)
        query, key, value = (mixture[:, (3 * g + i) * lane : (3 * g + i + 1) * lane] for i in range(3))
        query = query * (lax.rsqrt(jnp.sum(query * query, -1, keepdims=True) + eps_norm) * strength) + query_extra[...]
        key = key * lax.rsqrt(jnp.sum(key * key, -1, keepdims=True) + eps_norm) + key_extra[...] * strength
        out[g, 0] = query.astype(jnp.bfloat16)
        out[g, 1] = key.astype(jnp.bfloat16)
        out[g, 2] = (value + ones).astype(jnp.bfloat16)


def attend_kernel(own_count, own_masks, out_masks, size, gentle, scales, *refs):
    queries, parts, out, held = refs[:own_count], refs[own_count:-2], refs[-2], refs[-1]
    fast = all_gentle(scales) if gentle is None else None
    head = pl.program_id(0)
    heads = held.shape[0]
    piece_rows = out.shape[1]
    contract = (((1,), (1,)), ((), ()))

    def body(with_max):
        at = 0
        for own in queries:
            block = math.gcd(own.shape[2], 256)
            for begin in range(0, own.shape[2], block):
                query = own[0, 0, begin : begin + block, :]
                scores = [
                    lax.dot_general(query, part[0, 1], contract, preferred_element_type=jnp.float32) for part in parts
                ]
                if with_max:
                    strength = scales[0, head] * math.log2(math.e)
                    top = functools.reduce(jnp.maximum, [jnp.max(s, -1, keepdims=True) for s in scores])
                    scores = [(s - top) * strength for s in scores]
                mixed = sum(
                    jnp.dot(jnp.exp2(s).astype(jnp.bfloat16), part[0, 2], preferred_element_type=jnp.float32)
                    for s, part in zip(scores, parts)
                )
                held[head, at : at + block, :] = mixed[:, :size] / mixed[:, size : size + 1]
                at += block

    if gentle is None:
        pl.when(fast)(lambda: body(False))
        pl.when(jnp.logical_not(fast))(lambda: body(True))
    else:
        body(not gentle)

    @pl.when(head == heads - 1)
    def _():
        for j, mask in enumerate(out_masks):
            begin = own_masks.index(mask) * piece_rows
            out[j] = jnp.concatenate(
                [held[h, begin : begin + piece_rows, :] for h in range(heads)], -1
            ).astype(jnp.bfloat16)


def rows_kernel(level, shift, scale, out):
    out[0:1, :] = shift[pl.ds(level[0], 1), :]
    out[1:2, :] = scale[pl.ds(level[0], 1), :]


def mix_kernel(from_before, offsets, own, borrowed, out):
    rows, half, _ = own.shape
    lon = offsets[0, 1]
    column = lax.broadcasted_iota(jnp.int32, (half, 1), 0)
    far_side = column + half >= lon if from_before else column < lon
    for r in range(rows):
        out[r] = jnp.where(far_side, borrowed[r].astype(jnp.float32), own[r].astype(jnp.float32)).astype(jnp.bfloat16)


def finish_kernel(masks, level, tile, *refs):
    count = len(masks)
    places = places_of(masks)
    pieces, weight, gate, out = refs[:count], refs[count], refs[count + 1], refs[count + 2]
    inner = pieces[0].shape[-1]
    rows, half, _ = tile.shape
    total = 0.0
    for j in range(count):
        begin = pl.multiple_of(places[j] * inner, inner)
        total = total + jnp.dot(pieces[j][...], weight[pl.ds(begin, inner), :], preferred_element_type=jnp.float32)
    branch = gate[pl.ds(level[0], 1), :] * total.astype(jnp.bfloat16).astype(jnp.float32)
    for r in range(rows):
        out[r] = (tile[r].astype(jnp.float32) + branch[r * half : (r + 1) * half]).astype(jnp.bfloat16)


def assemble_kernel(offsets, local, mixed, moved, out):
    rows, half, _ = local.shape
    lon = offsets[0, 1]
    big = lon > half
    first = pl.multiple_of(jnp.where(big, 0, half), half)
    second = pl.multiple_of(jnp.where(big, half, 0), half)
    column = lax.broadcasted_iota(jnp.int32, (half, 1), 0) + second
    far_side = jnp.where(big, (column >= lon).astype(jnp.int32), (column < lon).astype(jnp.int32)) == 1
    out[0, :, pl.ds(first, half), :] = local[...]
    for r in range(rows):
        out[0, r, pl.ds(second, half), :] = jnp.where(
            far_side, moved[r].astype(jnp.float32), mixed[r].astype(jnp.float32)
        ).astype(jnp.bfloat16)


def shards(
    latents, timesteps, offsets, qkv_weight, logit_scale, out_weight, mod_shift, mod_scale, mod_gate
):
    tile = latents[0]
    rows, cols, width = tile.shape
    half = cols // 2
    heads = qkv_weight.shape[2]
    size = qkv_weight.shape[3] // 3
    inner = heads * size
    n = lax.axis_size("seq")
    masks = [0]
    bits = [1 << i for i in range(n.bit_length() - 1)]
    for bit in reversed(bits):
        masks = masks + [m | bit for m in masks]
    shift, scale, gate = mod_shift[0], mod_scale[0], mod_gate[0]
    piece_rows = rows * half
    half_tokens = n * piece_rows

    weight = jnp.transpose(qkv_weight[0], (1, 2, 0))
    group = 2 if heads % 2 == 0 else 1

    source_offsets = passed_along(offsets, "segment", 1)
    lon = offsets[0, 1]
    big = lon > half

    half_shape = jax.ShapeDtypeStruct((rows, half, width), jnp.bfloat16)

    def gathered(pieces):
        for bit in reversed(bits[:-1]):
            pieces = pieces + [swapped(p, "seq", bit) for p in pieces]
        return pieces

    def projected(pieces, held_masks, table_rows):
        tokens = len(pieces) * piece_rows
        return pl.pallas_call(
            functools.partial(project_kernel, held_masks, rows, size),
            grid=(heads // group,),
            out_shape=jax.ShapeDtypeStruct((heads, 3, tokens, lane), jnp.bfloat16),
            in_specs=[SMEM, SMEM]
            + [pl.BlockSpec((piece_rows, width), lambda h: (0, 0))] * len(pieces)
            + [pl.BlockSpec((group, 3 * size, width), lambda h: (h, 0, 0)), pl.BlockSpec((2, width), lambda h: (0, 0))],
            out_specs=pl.BlockSpec((group, 3, tokens, lane), lambda h: (h, 0, 0, 0)),
            scratch_shapes=[
                pltpu.VMEM((tokens, width), jnp.bfloat16),
                pltpu.VMEM((group * 3 * lane, width), jnp.bfloat16),
                pltpu.VMEM((tokens, lane), jnp.float32),
                pltpu.VMEM((tokens, lane), jnp.float32),
            ],
            compiler_params=params(),
            cost_estimate=small,
            name="project",
        )(offsets, logit_scale, *[p.reshape(piece_rows, width) for p in pieces], weight, table_rows)

    top = bits[-1]
    near_masks = gathered_masks([0], bits)
    far_masks = [m | top for m in near_masks]

    low, high = tile[:, :half], tile[:, half:]
    local = jnp.where(big, low, high)
    local_far = swapped(local, "seq", top)

    def mixed_half(from_before, low, high):
        own = high if from_before else low
        borrowed = passed_along(own, "win", 1 if from_before else -1)
        table_rows = pl.pallas_call(
            rows_kernel,
            out_shape=jax.ShapeDtypeStruct((2, width), jnp.float32),
            in_specs=[SMEM, VMEM, VMEM],
            out_specs=VMEM,
            compiler_params=params(),
            cost_estimate=small,
            name="rows",
        )(timesteps, shift, scale)
        near_heads = projected(gathered([low if from_before else high]), near_masks, table_rows)
        borrowed, near_heads = lax.optimization_barrier((borrowed, near_heads))
        mixed = pl.pallas_call(
            functools.partial(mix_kernel, from_before),
            out_shape=half_shape,
            in_specs=[SMEM, VMEM, VMEM],
            out_specs=VMEM,
            compiler_params=params(),
            cost_estimate=small,
            name="mix",
        )(offsets, own, borrowed)
        return mixed, near_heads, table_rows

    mixed, local_near, table_rows = lax.cond(
        big, functools.partial(mixed_half, True), functools.partial(mixed_half, False), low, high
    )
    local_far, mixed = lax.optimization_barrier((local_far, mixed))
    local_heads = [local_near, projected(gathered([local_far]), far_masks, table_rows)]
    mixed_far = swapped(mixed, "seq", top)
    near_heads = projected(gathered([mixed]), near_masks, table_rows)
    mixed_far, local_heads, near_heads, source_offsets = lax.optimization_barrier(
        (mixed_far, local_heads, near_heads, source_offsets)
    )
    far_heads = projected(gathered([mixed_far]), far_masks, table_rows)
    own_masks = near_masks + far_masks

    def attended(own, local_heads, gentle=None):
        def block(array, kinds):
            return pl.BlockSpec((1, kinds, array.shape[2], lane), lambda h: (h, 0, 0, 0))

        parts = [*local_heads, near_heads, far_heads]
        total = sum(o.shape[2] for o in own)
        return pl.pallas_call(
            functools.partial(attend_kernel, len(own), own_masks, masks, size, gentle),
            grid=(heads,),
            in_specs=[SMEM] + [block(o, 1) for o in own] + [block(p, 3) for p in parts],
            out_specs=pl.BlockSpec((n, piece_rows, inner), lambda h: (0, 0, 0)),
            scratch_shapes=[pltpu.VMEM((heads, total, size), jnp.float32)],
            out_shape=jax.ShapeDtypeStruct((n, piece_rows, inner), jnp.bfloat16),
            compiler_params=params(),
            cost_estimate=small,
            name="attend",
        )(logit_scale, *own, *parts)

    def hop(held, bit):
        middle = held.shape[1] // 2
        return held[:, :middle], swapped(held[:, middle:], "seq", bit)

    def returned(held):
        for bit in bits[1:]:
            held = jnp.concatenate(hop(held, bit), 0)
        return [held[g, 0] for g in range(n)]

    order = [0]
    for bit in bits:
        order = order + [m | bit for m in order]

    def finished(groups, residual):
        block = width // 3 if width % (3 * lane) == 0 else width
        sides = pl.BlockSpec((rows, half, block), lambda i: (0, 0, i))
        return pl.pallas_call(
            functools.partial(finish_kernel, order),
            grid=(width // block,),
            in_specs=[SMEM, sides]
            + [pl.BlockSpec((piece_rows, inner), lambda i: (0, 0))] * n
            + [pl.BlockSpec((width, block), lambda i: (0, i)), pl.BlockSpec((gate.shape[0], block), lambda i: (0, i))],
            out_specs=sides,
            out_shape=half_shape,
            compiler_params=params(),
            cost_estimate=small,
            name="finish",
        )(timesteps, residual, *groups, out_weight[0], gate)

    mixed_held = jnp.concatenate(
        hop(attended([near_heads, far_heads], local_heads)[None], bits[0]), 0
    )
    local_query, mixed_held = lax.optimization_barrier((local_heads, mixed_held))
    mixed_out = returned(mixed_held)
    local_attended = attended(local_query, local_query)
    local_kept, local_received = hop(local_attended[None], bits[0])
    mixed_done, local_received = lax.optimization_barrier((finished(mixed_out, mixed), local_received))
    mixed_sent = passed_along(mixed_done, "segment", 1)
    local_done = finished(returned(jnp.concatenate([local_kept, local_received], 0)), local)
    local_sent = passed_along(local_done, "segment", 1)
    mixed_sent, _ = lax.optimization_barrier((mixed_sent, local_done))
    moved = lax.cond(
        source_offsets[0, 1] > half,
        lambda block: passed_along(block, "win", -1),
        lambda block: passed_along(block, "win", 1),
        mixed_sent,
    )
    return pl.pallas_call(
        assemble_kernel,
        out_shape=jax.ShapeDtypeStruct((1, rows, cols, width), jnp.bfloat16),
        in_specs=[SMEM, VMEM, VMEM, VMEM],
        out_specs=VMEM,
        compiler_params=params(),
        cost_estimate=small,
        name="assemble",
    )(source_offsets, local_sent, mixed_sent, moved)


def solution(mesh):
    in_specs = (
        P("segment", "seq", "win", None),
        P("segment"),
        P("segment", None),
        P("segment", None, "seq", None),
        P("segment", "seq"),
        P("segment", None, None),
        P("segment", None, None),
        P("segment", None, None),
        P("segment", None, None),
    )
    out_specs = P("segment", "seq", "win", None)
    return jax.shard_map(shards, mesh=mesh, in_specs=in_specs, out_specs=out_specs, check_vma=False)
```

```python
import functools
import math

import jax
import jax.numpy as jnp
from jax import lax
from jax.experimental import pallas as pl
from jax.experimental.pallas import tpu as pltpu
from jax.sharding import PartitionSpec as P

eps_norm = 1e-06
lane = 128
far = 1e30
constant_shift_scale = 32.0

SMEM = pl.BlockSpec(memory_space=pltpu.SMEM)
VMEM = pl.BlockSpec(memory_space=pltpu.VMEM)


small = pl.CostEstimate(flops=1, bytes_accessed=1, transcendentals=0)


def params(mib=40):
    return pltpu.CompilerParams(vmem_limit_bytes=mib << 20)


def passed_along(block, axis, distance):
    n = lax.axis_size(axis)
    return lax.ppermute(block, axis, [(i, (i + distance) % n) for i in range(n)])


def swapped(block, axis, mask):
    return lax.ppermute(block, axis, [(i, i ^ mask) for i in range(lax.axis_size(axis))])


def places_of(masks):
    me = lax.axis_index("seq")
    return [me ^ m for m in masks]


def gathered_masks(held, bits):
    for bit in reversed(bits[:-1]):
        held = held + [m | bit for m in held]
    return held


def all_gentle(scales):
    top = scales[0, 0]
    for h in range(1, scales.shape[1]):
        top = jnp.maximum(top, scales[0, h])
    return top <= constant_shift_scale


def normalise(x, scale_row, shift_row):
    x = x - jnp.mean(x, -1, keepdims=True)
    variance = jnp.mean(x * x, -1, keepdims=True)
    return (x * lax.rsqrt(variance + eps_norm) * scale_row + shift_row).astype(jnp.bfloat16)


def project_kernel(masks, rows, size, offsets, scales, *refs):
    count = len(masks)
    places = places_of(masks)
    pieces = refs[:count]
    weight, rows_ref, out, tokens, padded, query_extra, key_extra = refs[count:]
    piece_rows = pieces[0].shape[0]
    half = piece_rows // rows
    group = weight.shape[0]
    step = pl.program_id(0)

    @pl.when(step == 0)
    def _():
        padded[...] = jnp.zeros_like(padded)
        shift_row, scale_row = rows_ref[0:1, :], rows_ref[1:2, :]
        column = lax.broadcasted_iota(jnp.int32, (piece_rows, lane), 1)
        local_row = lax.broadcasted_iota(jnp.int32, (piece_rows, lane), 0) // half
        chunk = math.gcd(piece_rows, 32)
        for j in range(count):
            for begin in range(0, piece_rows, chunk):
                x = pieces[j][begin : begin + chunk, :].astype(jnp.float32)
                at = j * piece_rows + begin
                tokens[at : at + chunk, :] = normalise(x, scale_row, shift_row)
            low = jnp.where(local_row + places[j] * rows < offsets[0, 0], 1.0, 0.0)
            span = slice(j * piece_rows, (j + 1) * piece_rows)
            query_extra[span, :] = jnp.where(
                column == size, low, jnp.where(column == size + 1, 1.0 - low, jnp.where(column == size + 2, 1.0, 0.0))
            )
            key_extra[span, :] = jnp.where(
                column == size,
                far * (low - 1.0),
                jnp.where(column == size + 1, -far * low, jnp.where(column == size + 2, -1.0, 0.0)),
            )

    for g in range(group):
        for i in range(3):
            begin = (3 * g + i) * lane
            padded[begin : begin + size, :] = weight[g, i * size : (i + 1) * size, :]
    mixture = lax.dot_general(
        tokens[...], padded[...], (((1,), (1,)), ((), ())), preferred_element_type=jnp.float32
    )
    ones = jnp.where(lax.broadcasted_iota(jnp.int32, (1, lane), 1) == size, 1.0, 0.0)
    fast = all_gentle(scales)
    for g in range(group):
        strength = jnp.where(fast, scales[0, step * group + g] * math.log2(math.e), 1.0)
        query, key, value = (mixture[:, (3 * g + i) * lane : (3 * g + i + 1) * lane] for i in range(3))
        query = query * (lax.rsqrt(jnp.sum(query * query, -1, keepdims=True) + eps_norm) * strength) + query_extra[...]
        key = key * lax.rsqrt(jnp.sum(key * key, -1, keepdims=True) + eps_norm) + key_extra[...] * strength
        out[g, 0] = query.astype(jnp.bfloat16)
        out[g, 1] = key.astype(jnp.bfloat16)
        out[g, 2] = (value + ones).astype(jnp.bfloat16)


def attend_kernel(own_count, own_masks, out_masks, size, scales, *refs):
    queries, parts, out, held = refs[:own_count], refs[own_count:-2], refs[-2], refs[-1]
    fast = all_gentle(scales)
    heads = held.shape[0]
    piece_rows = out.shape[1]
    contract = (((1,), (1,)), ((), ()))

    def body(with_max):
        for head in range(heads):
            at = 0
            for own in queries:
                block = math.gcd(own.shape[2], 256)
                for begin in range(0, own.shape[2], block):
                    query = own[head, 0, begin : begin + block, :]
                    scores = [
                        lax.dot_general(query, part[head, 1], contract, preferred_element_type=jnp.float32)
                        for part in parts
                    ]
                    if with_max:
                        strength = scales[0, head] * math.log2(math.e)
                        top = functools.reduce(jnp.maximum, [jnp.max(s, -1, keepdims=True) for s in scores])
                        scores = [(s - top) * strength for s in scores]
                    mixed = sum(
                        jnp.dot(jnp.exp2(s).astype(jnp.bfloat16), part[head, 2], preferred_element_type=jnp.float32)
                        for s, part in zip(scores, parts)
                    )
                    held[head, at : at + block, :] = mixed[:, :size] / mixed[:, size : size + 1]
                    at += block

    pl.when(fast)(lambda: body(False))
    pl.when(jnp.logical_not(fast))(lambda: body(True))
    for j, mask in enumerate(out_masks):
        begin = own_masks.index(mask) * piece_rows
        out[j] = jnp.concatenate([held[h, begin : begin + piece_rows, :] for h in range(heads)], -1).astype(
            jnp.bfloat16
        )


def rows_kernel(level, shift, scale, out):
    out[0:1, :] = shift[pl.ds(level[0], 1), :]
    out[1:2, :] = scale[pl.ds(level[0], 1), :]


def mix_kernel(from_before, offsets, own, borrowed, out):
    rows, half, _ = own.shape
    lon = offsets[0, 1]
    column = lax.broadcasted_iota(jnp.int32, (half, 1), 0)
    far_side = column + half >= lon if from_before else column < lon
    for r in range(rows):
        out[r] = jnp.where(far_side, borrowed[r].astype(jnp.float32), own[r].astype(jnp.float32)).astype(jnp.bfloat16)


def finish_kernel(masks, level, tile, *refs):
    count = len(masks)
    places = places_of(masks)
    pieces, weight, gate, out = refs[:count], refs[count], refs[count + 1], refs[count + 2]
    inner = pieces[0].shape[-1]
    rows, half, _ = tile.shape
    total = 0.0
    for j in range(count):
        begin = pl.multiple_of(places[j] * inner, inner)
        total = total + jnp.dot(pieces[j][...], weight[pl.ds(begin, inner), :], preferred_element_type=jnp.float32)
    branch = gate[pl.ds(level[0], 1), :] * total.astype(jnp.bfloat16).astype(jnp.float32)
    for r in range(rows):
        out[r] = (tile[r].astype(jnp.float32) + branch[r * half : (r + 1) * half]).astype(jnp.bfloat16)


def assemble_kernel(offsets, local, mixed, moved, out):
    rows, half, _ = local.shape
    lon = offsets[0, 1]
    big = lon > half
    first = pl.multiple_of(jnp.where(big, 0, half), half)
    second = pl.multiple_of(jnp.where(big, half, 0), half)
    column = lax.broadcasted_iota(jnp.int32, (half, 1), 0) + second
    far_side = jnp.where(big, (column >= lon).astype(jnp.int32), (column < lon).astype(jnp.int32)) == 1
    out[0, :, pl.ds(first, half), :] = local[...]
    for r in range(rows):
        out[0, r, pl.ds(second, half), :] = jnp.where(
            far_side, moved[r].astype(jnp.float32), mixed[r].astype(jnp.float32)
        ).astype(jnp.bfloat16)


def shards(
    latents, timesteps, offsets, qkv_weight, logit_scale, out_weight, mod_shift, mod_scale, mod_gate
):
    tile = latents[0]
    rows, cols, width = tile.shape
    half = cols // 2
    heads = qkv_weight.shape[2]
    size = qkv_weight.shape[3] // 3
    inner = heads * size
    n = lax.axis_size("seq")
    masks = [0]
    bits = [1 << i for i in range(n.bit_length() - 1)]
    for bit in reversed(bits):
        masks = masks + [m | bit for m in masks]
    shift, scale, gate = mod_shift[0], mod_scale[0], mod_gate[0]
    piece_rows = rows * half
    half_tokens = n * piece_rows

    weight = jnp.transpose(qkv_weight[0], (1, 2, 0))
    group = 2 if heads % 2 == 0 else 1

    source_offsets = passed_along(offsets, "segment", 1)
    lon = offsets[0, 1]
    big = lon > half

    half_shape = jax.ShapeDtypeStruct((rows, half, width), jnp.bfloat16)

    def gathered(pieces):
        for bit in reversed(bits[:-1]):
            pieces = pieces + [swapped(p, "seq", bit) for p in pieces]
        return pieces

    def projected(pieces, held_masks, table_rows):
        tokens = len(pieces) * piece_rows
        return pl.pallas_call(
            functools.partial(project_kernel, held_masks, rows, size),
            grid=(heads // group,),
            out_shape=jax.ShapeDtypeStruct((heads, 3, tokens, lane), jnp.bfloat16),
            in_specs=[SMEM, SMEM]
            + [pl.BlockSpec((piece_rows, width), lambda h: (0, 0))] * len(pieces)
            + [pl.BlockSpec((group, 3 * size, width), lambda h: (h, 0, 0)), pl.BlockSpec((2, width), lambda h: (0, 0))],
            out_specs=pl.BlockSpec((group, 3, tokens, lane), lambda h: (h, 0, 0, 0)),
            scratch_shapes=[
                pltpu.VMEM((tokens, width), jnp.bfloat16),
                pltpu.VMEM((group * 3 * lane, width), jnp.bfloat16),
                pltpu.VMEM((tokens, lane), jnp.float32),
                pltpu.VMEM((tokens, lane), jnp.float32),
            ],
            compiler_params=params(),
            cost_estimate=small,
            name="project",
        )(offsets, logit_scale, *[p.reshape(piece_rows, width) for p in pieces], weight, table_rows)

    top = bits[-1]
    near_masks = gathered_masks([0], bits)
    far_masks = [m | top for m in near_masks]

    low, high = tile[:, :half], tile[:, half:]
    local = jnp.where(big, low, high)
    local_far = swapped(local, "seq", top)

    def mixed_half(from_before, low, high):
        own = high if from_before else low
        borrowed = passed_along(own, "win", 1 if from_before else -1)
        table_rows = pl.pallas_call(
            rows_kernel,
            out_shape=jax.ShapeDtypeStruct((2, width), jnp.float32),
            in_specs=[SMEM, VMEM, VMEM],
            out_specs=VMEM,
            compiler_params=params(),
            cost_estimate=small,
            name="rows",
        )(timesteps, shift, scale)
        near_heads = projected(gathered([low if from_before else high]), near_masks, table_rows)
        borrowed, near_heads = lax.optimization_barrier((borrowed, near_heads))
        mixed = pl.pallas_call(
            functools.partial(mix_kernel, from_before),
            out_shape=half_shape,
            in_specs=[SMEM, VMEM, VMEM],
            out_specs=VMEM,
            compiler_params=params(),
            cost_estimate=small,
            name="mix",
        )(offsets, own, borrowed)
        return mixed, near_heads, table_rows

    mixed, local_near, table_rows = lax.cond(
        big, functools.partial(mixed_half, True), functools.partial(mixed_half, False), low, high
    )
    local_far, mixed = lax.optimization_barrier((local_far, mixed))
    local_heads = [local_near, projected(gathered([local_far]), far_masks, table_rows)]
    mixed_far = swapped(mixed, "seq", top)
    near_heads = projected(gathered([mixed]), near_masks, table_rows)
    mixed_far, local_heads, near_heads, source_offsets = lax.optimization_barrier(
        (mixed_far, local_heads, near_heads, source_offsets)
    )
    far_heads = projected(gathered([mixed_far]), far_masks, table_rows)
    own_masks = near_masks + far_masks

    def attended(own, local_heads):
        parts = [*local_heads, near_heads, far_heads]
        total = sum(o.shape[2] for o in own)
        return pl.pallas_call(
            functools.partial(attend_kernel, len(own), own_masks, masks, size),
            in_specs=[SMEM] + [VMEM] * (len(own) + len(parts)),
            out_specs=VMEM,
            scratch_shapes=[pltpu.VMEM((heads, total, size), jnp.float32)],
            out_shape=jax.ShapeDtypeStruct((n, piece_rows, inner), jnp.bfloat16),
            compiler_params=params(),
            cost_estimate=small,
            name="attend",
        )(logit_scale, *own, *parts)

    def hop(held, bit):
        middle = held.shape[1] // 2
        return held[:, :middle], swapped(held[:, middle:], "seq", bit)

    def returned(held):
        for bit in bits[1:]:
            held = jnp.concatenate(hop(held, bit), 0)
        return [held[g, 0] for g in range(n)]

    order = [0]
    for bit in bits:
        order = order + [m | bit for m in order]

    def finished(groups, residual):
        block = width // 3 if width % (3 * lane) == 0 else width
        sides = pl.BlockSpec((rows, half, block), lambda i: (0, 0, i))
        return pl.pallas_call(
            functools.partial(finish_kernel, order),
            grid=(width // block,),
            in_specs=[SMEM, sides]
            + [pl.BlockSpec((piece_rows, inner), lambda i: (0, 0))] * n
            + [pl.BlockSpec((width, block), lambda i: (0, i)), pl.BlockSpec((gate.shape[0], block), lambda i: (0, i))],
            out_specs=sides,
            out_shape=half_shape,
            compiler_params=params(),
            cost_estimate=small,
            name="finish",
        )(timesteps, residual, *groups, out_weight[0], gate)

    mixed_held = jnp.concatenate(
        hop(attended([near_heads, far_heads], local_heads)[None], bits[0]), 0
    )
    local_query, mixed_held = lax.optimization_barrier((local_heads, mixed_held))
    mixed_out = returned(mixed_held)
    local_attended = attended(local_query, local_query)
    local_kept, local_received = hop(local_attended[None], bits[0])
    mixed_done, local_received = lax.optimization_barrier((finished(mixed_out, mixed), local_received))
    mixed_sent = passed_along(mixed_done, "segment", 1)
    local_done = finished(returned(jnp.concatenate([local_kept, local_received], 0)), local)
    local_sent = passed_along(local_done, "segment", 1)
    mixed_sent, _ = lax.optimization_barrier((mixed_sent, local_done))
    moved = lax.cond(
        source_offsets[0, 1] > half,
        lambda block: passed_along(block, "win", -1),
        lambda block: passed_along(block, "win", 1),
        mixed_sent,
    )
    block = math.gcd(rows, 4)
    piece = pl.BlockSpec((block, half, width), lambda i: (i, 0, 0))
    return pl.pallas_call(
        assemble_kernel,
        grid=(rows // block,),
        out_shape=jax.ShapeDtypeStruct((1, rows, cols, width), jnp.bfloat16),
        in_specs=[SMEM, piece, piece, piece],
        out_specs=pl.BlockSpec((1, block, cols, width), lambda i: (0, i, 0, 0)),
        compiler_params=params(),
        cost_estimate=small,
        name="assemble",
    )(source_offsets, local_sent, mixed_sent, moved)


def solution(mesh):
    in_specs = (
        P("segment", "seq", "win", None),
        P("segment"),
        P("segment", None),
        P("segment", None, "seq", None),
        P("segment", "seq"),
        P("segment", None, None),
        P("segment", None, None),
        P("segment", None, None),
        P("segment", None, None),
    )
    out_specs = P("segment", "seq", "win", None)
    return jax.shard_map(shards, mesh=mesh, in_specs=in_specs, out_specs=out_specs, check_vma=False)
```

```python
import functools
import math

import jax
import jax.numpy as jnp
from jax import lax
from jax.experimental import pallas as pl
from jax.experimental.pallas import tpu as pltpu
from jax.sharding import PartitionSpec as P

eps_norm = 1e-06
lane = 128
far = 1e30
constant_shift_scale = 32.0

SMEM = pl.BlockSpec(memory_space=pltpu.SMEM)
VMEM = pl.BlockSpec(memory_space=pltpu.VMEM)


small = pl.CostEstimate(flops=1, bytes_accessed=1, transcendentals=0)


def params(mib=40):
    return pltpu.CompilerParams(vmem_limit_bytes=mib << 20)


def passed_along(block, axis, distance):
    n = lax.axis_size(axis)
    return lax.ppermute(block, axis, [(i, (i + distance) % n) for i in range(n)])


def swapped(block, axis, mask):
    return lax.ppermute(block, axis, [(i, i ^ mask) for i in range(lax.axis_size(axis))])


def places_of(masks):
    me = lax.axis_index("seq")
    return [me ^ m for m in masks]


def gathered_masks(held, bits):
    for bit in reversed(bits[:-1]):
        held = held + [m | bit for m in held]
    return held


def all_gentle(scales):
    top = scales[0, 0]
    for h in range(1, scales.shape[1]):
        top = jnp.maximum(top, scales[0, h])
    return top <= constant_shift_scale


def normalise(x, scale_row, shift_row):
    x = x - jnp.mean(x, -1, keepdims=True)
    variance = jnp.mean(x * x, -1, keepdims=True)
    return (x * lax.rsqrt(variance + eps_norm) * scale_row + shift_row).astype(jnp.bfloat16)


def project_kernel(masks, rows, size, offsets, scales, *refs):
    count = len(masks)
    places = places_of(masks)
    pieces = refs[:count]
    weight, rows_ref, out, tokens, padded, query_extra, key_extra = refs[count:]
    piece_rows = pieces[0].shape[0]
    half = piece_rows // rows
    group = weight.shape[0]
    step = pl.program_id(0)

    @pl.when(step == 0)
    def _():
        padded[...] = jnp.zeros_like(padded)
        shift_row, scale_row = rows_ref[0:1, :], rows_ref[1:2, :]
        column = lax.broadcasted_iota(jnp.int32, (piece_rows, lane), 1)
        local_row = lax.broadcasted_iota(jnp.int32, (piece_rows, lane), 0) // half
        chunk = math.gcd(piece_rows, 32)
        for j in range(count):
            for begin in range(0, piece_rows, chunk):
                x = pieces[j][begin : begin + chunk, :].astype(jnp.float32)
                at = j * piece_rows + begin
                tokens[at : at + chunk, :] = normalise(x, scale_row, shift_row)
            low = jnp.where(local_row + places[j] * rows < offsets[0, 0], 1.0, 0.0)
            span = slice(j * piece_rows, (j + 1) * piece_rows)
            query_extra[span, :] = jnp.where(
                column == size, low, jnp.where(column == size + 1, 1.0 - low, jnp.where(column == size + 2, 1.0, 0.0))
            )
            key_extra[span, :] = jnp.where(
                column == size,
                far * (low - 1.0),
                jnp.where(column == size + 1, -far * low, jnp.where(column == size + 2, -1.0, 0.0)),
            )

    for g in range(group):
        for i in range(3):
            begin = (3 * g + i) * lane
            padded[begin : begin + size, :] = weight[g, i * size : (i + 1) * size, :]
    mixture = lax.dot_general(
        tokens[...], padded[...], (((1,), (1,)), ((), ())), preferred_element_type=jnp.float32
    )
    ones = jnp.where(lax.broadcasted_iota(jnp.int32, (1, lane), 1) == size, 1.0, 0.0)
    fast = all_gentle(scales)
    for g in range(group):
        strength = jnp.where(fast, scales[0, step * group + g] * math.log2(math.e), 1.0)
        query, key, value = (mixture[:, (3 * g + i) * lane : (3 * g + i + 1) * lane] for i in range(3))
        query = query * (lax.rsqrt(jnp.sum(query * query, -1, keepdims=True) + eps_norm) * strength) + query_extra[...]
        key = key * lax.rsqrt(jnp.sum(key * key, -1, keepdims=True) + eps_norm) + key_extra[...] * strength
        out[g, 0] = query.astype(jnp.bfloat16)
        out[g, 1] = key.astype(jnp.bfloat16)
        out[g, 2] = (value + ones).astype(jnp.bfloat16)


def attend_kernel(own_count, own_masks, out_masks, size, scales, *refs):
    queries, parts, out, held = refs[:own_count], refs[own_count:-2], refs[-2], refs[-1]
    fast = all_gentle(scales)
    heads = held.shape[0]
    piece_rows = out.shape[1]
    contract = (((1,), (1,)), ((), ()))

    def body(with_max):
        for head in range(heads):
            at = 0
            for own in queries:
                block = math.gcd(own.shape[2], 256)
                for begin in range(0, own.shape[2], block):
                    query = own[head, 0, begin : begin + block, :]
                    scores = [
                        lax.dot_general(query, part[head, 1], contract, preferred_element_type=jnp.float32)
                        for part in parts
                    ]
                    if with_max:
                        strength = scales[0, head] * math.log2(math.e)
                        top = functools.reduce(jnp.maximum, [jnp.max(s, -1, keepdims=True) for s in scores])
                        scores = [(s - top) * strength for s in scores]
                    mixed = sum(
                        jnp.dot(jnp.exp2(s).astype(jnp.bfloat16), part[head, 2], preferred_element_type=jnp.float32)
                        for s, part in zip(scores, parts)
                    )
                    held[head, at : at + block, :] = mixed[:, :size] / mixed[:, size : size + 1]
                    at += block

    pl.when(fast)(lambda: body(False))
    pl.when(jnp.logical_not(fast))(lambda: body(True))
    for j, mask in enumerate(out_masks):
        begin = own_masks.index(mask) * piece_rows
        out[j] = jnp.concatenate([held[h, begin : begin + piece_rows, :] for h in range(heads)], -1).astype(
            jnp.bfloat16
        )


def rows_kernel(level, shift, scale, out):
    out[0:1, :] = shift[pl.ds(level[0], 1), :]
    out[1:2, :] = scale[pl.ds(level[0], 1), :]


def mix_kernel(from_before, offsets, own, borrowed, out):
    rows, half, _ = own.shape
    lon = offsets[0, 1]
    column = lax.broadcasted_iota(jnp.int32, (half, 1), 0)
    far_side = column + half >= lon if from_before else column < lon
    for r in range(rows):
        out[r] = jnp.where(far_side, borrowed[r].astype(jnp.float32), own[r].astype(jnp.float32)).astype(jnp.bfloat16)


def finish_kernel(masks, level, tile, *refs):
    count = len(masks)
    places = places_of(masks)
    pieces, weight, gate, out = refs[:count], refs[count], refs[count + 1], refs[count + 2]
    inner = pieces[0].shape[-1]
    rows, half, _ = tile.shape
    total = 0.0
    for j in range(count):
        begin = pl.multiple_of(places[j] * inner, inner)
        total = total + jnp.dot(pieces[j][...], weight[pl.ds(begin, inner), :], preferred_element_type=jnp.float32)
    branch = gate[pl.ds(level[0], 1), :] * total.astype(jnp.bfloat16).astype(jnp.float32)
    for r in range(rows):
        out[r] = (tile[r].astype(jnp.float32) + branch[r * half : (r + 1) * half]).astype(jnp.bfloat16)


def assemble_kernel(offsets, local, mixed, moved, out):
    rows, half, _ = local.shape
    lon = offsets[0, 1]
    big = lon > half
    first = pl.multiple_of(jnp.where(big, 0, half), half)
    second = pl.multiple_of(jnp.where(big, half, 0), half)
    column = lax.broadcasted_iota(jnp.int32, (half, 1), 0) + second
    far_side = jnp.where(big, (column >= lon).astype(jnp.int32), (column < lon).astype(jnp.int32)) == 1
    out[0, :, pl.ds(first, half), :] = local[...]
    for r in range(rows):
        out[0, r, pl.ds(second, half), :] = jnp.where(
            far_side, moved[r].astype(jnp.float32), mixed[r].astype(jnp.float32)
        ).astype(jnp.bfloat16)


def shards(
    latents, timesteps, offsets, qkv_weight, logit_scale, out_weight, mod_shift, mod_scale, mod_gate
):
    tile = latents[0]
    rows, cols, width = tile.shape
    half = cols // 2
    heads = qkv_weight.shape[2]
    size = qkv_weight.shape[3] // 3
    inner = heads * size
    n = lax.axis_size("seq")
    masks = [0]
    bits = [1 << i for i in range(n.bit_length() - 1)]
    for bit in reversed(bits):
        masks = masks + [m | bit for m in masks]
    shift, scale, gate = mod_shift[0], mod_scale[0], mod_gate[0]
    piece_rows = rows * half
    half_tokens = n * piece_rows

    weight = jnp.transpose(qkv_weight[0], (1, 2, 0))
    group = 2 if heads % 2 == 0 else 1

    source_offsets = passed_along(offsets, "segment", 1)
    lon = offsets[0, 1]
    big = lon > half

    half_shape = jax.ShapeDtypeStruct((rows, half, width), jnp.bfloat16)

    def gathered(pieces):
        for bit in reversed(bits[:-1]):
            pieces = pieces + [swapped(p, "seq", bit) for p in pieces]
        return pieces

    def projected(pieces, held_masks, table_rows):
        tokens = len(pieces) * piece_rows
        return pl.pallas_call(
            functools.partial(project_kernel, held_masks, rows, size),
            grid=(heads // group,),
            out_shape=jax.ShapeDtypeStruct((heads, 3, tokens, lane), jnp.bfloat16),
            in_specs=[SMEM, SMEM]
            + [pl.BlockSpec((piece_rows, width), lambda h: (0, 0))] * len(pieces)
            + [pl.BlockSpec((group, 3 * size, width), lambda h: (h, 0, 0)), pl.BlockSpec((2, width), lambda h: (0, 0))],
            out_specs=pl.BlockSpec((group, 3, tokens, lane), lambda h: (h, 0, 0, 0)),
            scratch_shapes=[
                pltpu.VMEM((tokens, width), jnp.bfloat16),
                pltpu.VMEM((group * 3 * lane, width), jnp.bfloat16),
                pltpu.VMEM((tokens, lane), jnp.float32),
                pltpu.VMEM((tokens, lane), jnp.float32),
            ],
            compiler_params=params(),
            cost_estimate=small,
            name="project",
        )(offsets, logit_scale, *[p.reshape(piece_rows, width) for p in pieces], weight, table_rows)

    top = bits[-1]
    near_masks = gathered_masks([0], bits)
    far_masks = [m | top for m in near_masks]

    low, high = tile[:, :half], tile[:, half:]
    local = jnp.where(big, low, high)
    local_far = swapped(local, "seq", top)

    def mixed_half(from_before, low, high):
        own = high if from_before else low
        borrowed = passed_along(own, "win", 1 if from_before else -1)
        table_rows = pl.pallas_call(
            rows_kernel,
            out_shape=jax.ShapeDtypeStruct((2, width), jnp.float32),
            in_specs=[SMEM, VMEM, VMEM],
            out_specs=VMEM,
            compiler_params=params(),
            cost_estimate=small,
            name="rows",
        )(timesteps, shift, scale)
        near_heads = projected(gathered([low if from_before else high]), near_masks, table_rows)
        borrowed, near_heads = lax.optimization_barrier((borrowed, near_heads))
        mixed = pl.pallas_call(
            functools.partial(mix_kernel, from_before),
            out_shape=half_shape,
            in_specs=[SMEM, VMEM, VMEM],
            out_specs=VMEM,
            compiler_params=params(),
            cost_estimate=small,
            name="mix",
        )(offsets, own, borrowed)
        return mixed, near_heads, table_rows

    mixed, local_near, table_rows = lax.cond(
        big, functools.partial(mixed_half, True), functools.partial(mixed_half, False), low, high
    )
    local_far, mixed = lax.optimization_barrier((local_far, mixed))
    local_heads = [local_near, projected(gathered([local_far]), far_masks, table_rows)]
    mixed_far = swapped(mixed, "seq", top)
    near_heads = projected(gathered([mixed]), near_masks, table_rows)
    mixed_far, local_heads, near_heads, source_offsets = lax.optimization_barrier(
        (mixed_far, local_heads, near_heads, source_offsets)
    )
    far_heads = projected(gathered([mixed_far]), far_masks, table_rows)
    own_masks = near_masks + far_masks

    def attended(own, local_heads):
        parts = [*local_heads, near_heads, far_heads]
        total = sum(o.shape[2] for o in own)
        return pl.pallas_call(
            functools.partial(attend_kernel, len(own), own_masks, masks, size),
            in_specs=[SMEM] + [VMEM] * (len(own) + len(parts)),
            out_specs=VMEM,
            scratch_shapes=[pltpu.VMEM((heads, total, size), jnp.float32)],
            out_shape=jax.ShapeDtypeStruct((n, piece_rows, inner), jnp.bfloat16),
            compiler_params=params(),
            cost_estimate=small,
            name="attend",
        )(logit_scale, *own, *parts)

    def hop(held, bit):
        middle = held.shape[1] // 2
        return held[:, :middle], swapped(held[:, middle:], "seq", bit)

    def returned(held):
        for bit in bits[1:]:
            held = jnp.concatenate(hop(held, bit), 0)
        return [held[g, 0] for g in range(n)]

    order = [0]
    for bit in bits:
        order = order + [m | bit for m in order]

    def finished(groups, residual):
        block = width // 3 if width % (3 * lane) == 0 else width
        sides = pl.BlockSpec((rows, half, block), lambda i: (0, 0, i))
        return pl.pallas_call(
            functools.partial(finish_kernel, order),
            grid=(width // block,),
            in_specs=[SMEM, sides]
            + [pl.BlockSpec((piece_rows, inner), lambda i: (0, 0))] * n
            + [pl.BlockSpec((width, block), lambda i: (0, i)), pl.BlockSpec((gate.shape[0], block), lambda i: (0, i))],
            out_specs=sides,
            out_shape=half_shape,
            compiler_params=params(),
            cost_estimate=small,
            name="finish",
        )(timesteps, residual, *groups, out_weight[0], gate)

    mixed_held = jnp.concatenate(
        hop(attended([near_heads, far_heads], local_heads)[None], bits[0]), 0
    )
    local_query, mixed_held = lax.optimization_barrier((local_heads, mixed_held))
    mixed_out = returned(mixed_held)
    local_attended = attended(local_query, local_query)
    local_kept, local_received = hop(local_attended[None], bits[0])
    mixed_done = finished(mixed_out, mixed)
    mixed_sent = passed_along(mixed_done, "segment", 1)
    local_done = finished(returned(jnp.concatenate([local_kept, local_received], 0)), local)
    local_sent = passed_along(local_done, "segment", 1)
    mixed_sent, _ = lax.optimization_barrier((mixed_sent, local_done))
    moved = lax.cond(
        source_offsets[0, 1] > half,
        lambda block: passed_along(block, "win", -1),
        lambda block: passed_along(block, "win", 1),
        mixed_sent,
    )
    block = math.gcd(rows, 4)
    piece = pl.BlockSpec((block, half, width), lambda i: (i, 0, 0))
    return pl.pallas_call(
        assemble_kernel,
        grid=(rows // block,),
        out_shape=jax.ShapeDtypeStruct((1, rows, cols, width), jnp.bfloat16),
        in_specs=[SMEM, piece, piece, piece],
        out_specs=pl.BlockSpec((1, block, cols, width), lambda i: (0, i, 0, 0)),
        compiler_params=params(),
        cost_estimate=small,
        name="assemble",
    )(source_offsets, local_sent, mixed_sent, moved)


def solution(mesh):
    in_specs = (
        P("segment", "seq", "win", None),
        P("segment"),
        P("segment", None),
        P("segment", None, "seq", None),
        P("segment", "seq"),
        P("segment", None, None),
        P("segment", None, None),
        P("segment", None, None),
        P("segment", None, None),
    )
    out_specs = P("segment", "seq", "win", None)
    return jax.shard_map(shards, mesh=mesh, in_specs=in_specs, out_specs=out_specs, check_vma=False)
```
